256 devices in a mesh: slab: 4 (over x), tile: 64 (over z, y, core).
Axes of the slice: x: 4, y: 4, z: 8, core: 2. Of those that a mesh axis runs over, the one named last changes fastest.
Arguments:
- distributions: float32 [7, 128, 256, 256], P(None, 'slab', 'tile'), may hold values from 0 to 0.3
- gate_states: float32 [3, 128, 256, 256], P(None, 'slab', 'tile'), may hold values from 0 to 1
- history: float32 [32, 128, 256, 256], P(None, 'slab', 'tile')
- tissue: int32 [128, 256, 256], P('slab', 'tile'), may hold values from 0 to 3, as said below
- stim_site: int32 [128, 256, 256], P('slab', 'tile'), may hold values from 0 to 8, as said below
- stim_amp: float32 [8], replicated, may hold values from 1 to 10
- record_column: int32 [2], replicated, may hold values from 0 to 31, as said below
Outputs:
- next_distributions: float32 [7, 128, 256, 256], P(None, 'slab', 'tile')
- next_gates: float32 [3, 128, 256, 256], P(None, 'slab', 'tile')
- pod_basis: float32 [32, 128, 256, 256], P(None, 'slab', 'tile')
- upper_factor: float32 [32, 32], replicated
The draws below stay inside these ranges and needn't reach their ends.
Inputs may be any that keep to these rules, and one draw needn't show every extreme that they name: `tissue`: 0 outside the heart or in a gap; 1 endocardial, 2 midmyocardial, 3 epicardial cells. `stim_site`: 0 means no stimulus; k > 0 drives the voxel with stim_amp[k - 1]. `record_column`: distinct column indices; one of them is the last column.
All inputs are finite; a program needn't handle non-finite values.
Results may differ from the reference program's by a relative error of at most 0.0003.
Values sent between devices are 32-bit elements; how exact they have to be, the bound alone decides.
A program may use at most 128 MiB of HBM per device.

```python
import math
import jax
import jax.numpy as jnp
from jax import lax

SNAP = 32
STEPS = 2
STIM = 8
NX = 128
NY = 256
NZ = 256


def draw_history(key, part):
    keys = jax.random.split(key, 4)
    shape = (SNAP, NX, NY, NZ)
    column_scale = jnp.exp(jax.random.uniform(keys[1], (SNAP, 1, 1, 1), jnp.float32) * math.log(10.0))
    row_scale = jnp.exp(jax.random.uniform(keys[2], (1, NX, NY, NZ), jnp.float32) * math.log(10.0))
    along_x = lax.broadcasted_iota(jnp.float32, (1, NX, NY, NZ), 1) / NX
    along_y = lax.broadcasted_iota(jnp.float32, (1, NX, NY, NZ), 2) / NY
    rising = jnp.exp(math.log(3.0) * (along_x + along_y))
    common = jax.random.normal(keys[3], (1, NX, NY, NZ), jnp.float32)
    values = (0.03 * jax.random.normal(keys[0], shape, jnp.float32) + common) * rising
    return values * column_scale * row_scale * 0.05


def draw_tissue(key, part):
    keys = jax.random.split(key, 2)
    coord_x = lax.broadcasted_iota(jnp.int32, (NX, NY, NZ), 0)
    coord_y = lax.broadcasted_iota(jnp.int32, (NX, NY, NZ), 1)
    coord_z = lax.broadcasted_iota(jnp.int32, (NX, NY, NZ), 2)
    reach_x = (2 * coord_x + 1 - NX) * 64 // NX
    reach_y = (2 * coord_y + 1 - NY) * 64 // NY
    reach_z = (2 * coord_z + 1 - NZ) * 64 // NZ
    inside = reach_x * reach_x + reach_y * reach_y + reach_z * reach_z < 9000
    kept = jax.random.randint(keys[0], (NX, NY, NZ), 0, 10) != 0
    kind = jax.random.randint(keys[1], (NX, NY, NZ), 1, 4)
    return jnp.where(inside & kept, kind, 0).astype(jnp.int32)


def draw_stim_site(key, part):
    keys = jax.random.split(key, 2)
    chosen = jax.random.randint(keys[0], (NX, NY, NZ), 0, 16) == 0
    which = jax.random.randint(keys[1], (NX, NY, NZ), 1, STIM + 1)
    return jnp.where(chosen, which, 0).astype(jnp.int32)


def draw_record_column(key, part):
    others = jax.random.permutation(jax.random.fold_in(key, 7), SNAP - 1)[:STEPS - 1]
    picked = jnp.concatenate([jnp.full((1,), SNAP - 1, jnp.int32), others.astype(jnp.int32)])
    order = jax.random.permutation(jax.random.fold_in(key, 11), STEPS)
    return picked[order].astype(jnp.int32)


def block_scale(rng, dims, cuts, smallest, high):
    loudness, own = 1.0, jax.random.fold_in(rng, 6)
    for position, shards_of in cuts:
        steps = jnp.exp(jax.random.uniform(jax.random.fold_in(own, position), (shards_of,), jnp.float32, smallest / len(cuts), high / len(cuts)))
        loudness = loudness * jnp.repeat(steps, dims[position] // shards_of).reshape([-1 if axis == position else 1 for axis in range(len(dims))])
    return loudness


def setup_inputs(seed: int = 0) -> dict:
    streams_of = jax.random.split(jax.random.key(seed), 8)
    return {
        "distributions": jnp.clip(0.3 * jax.random.uniform(streams_of[0], (7, NX, NY, NZ), jnp.float32) ** block_scale(streams_of[0], (7, NX, NY, NZ), ((1, 4), (2, 64)), -0.2, 0.2), 0.0, 0.3),
        "gate_states": jnp.clip(1.0 * jax.random.uniform(streams_of[1], (3, NX, NY, NZ), jnp.float32) ** block_scale(streams_of[1], (3, NX, NY, NZ), ((1, 4), (2, 64)), -0.2, 0.2), 0.0, 1.0),
        "history": draw_history(jax.random.fold_in(streams_of[7], 71), 0),
        "tissue": draw_tissue(jax.random.fold_in(streams_of[7], 71), 0),
        "stim_site": draw_stim_site(jax.random.fold_in(streams_of[7], 71), 0),
        "stim_amp": jnp.clip(jnp.exp(jax.random.uniform(streams_of[5], (STIM,), jnp.float32, math.log(1.0), math.log(10.0))), 1.0, 10.0),
        "record_column": draw_record_column(jax.random.fold_in(streams_of[7], 71), 0),
    }


STEP_TIME = 0.1
SHARPNESS = 50.0
LATTICE_WEIGHTS = (0.25, 0.125, 0.125, 0.125, 0.125, 0.125, 0.125)
VELOCITIES = ((0, 0, 0), (1, 0, 0), (-1, 0, 0), (0, 1, 0), (0, -1, 0), (0, 0, 1), (0, 0, -1))
OPPOSITE = (0, 2, 1, 4, 3, 6, 5)
TYPE_TABLE = {'relax_time': (0.95, 0.8, 1.1), 'u_upper': (1.56, 1.61, 1.55), 'theta_vminus': (0.2, 0.1, 0.006), 'theta_zero': (0.006, 0.005, 0.006), 'tau_v1minus': (75.0, 80.0, 60.0), 'tau_v2minus': (10.0, 1.4506, 1150.0), 'tau_w1minus': (6.0, 70.0, 60.0), 'tau_w2minus': (140.0, 8.0, 15.0), 'k_wminus': (200.0, 200.0, 65.0), 'u_wminus': (0.016, 0.016, 0.03), 'tau_wplus': (280.0, 280.0, 200.0), 'tau_fast': (0.1, 0.078, 0.11), 'tau_o1': (470.0, 410.0, 400.0), 'tau_o2': (6.0, 7.0, 6.0), 'tau_so1': (40.0, 91.0, 30.0181), 'tau_so2': (1.2, 0.8, 0.9957), 'k_so': (2.0, 2.1, 2.0458), 'u_so': (0.65, 0.6, 0.65), 'tau_s2': (2.0, 4.0, 16.0), 'tau_slow': (2.9013, 3.3849, 1.8875), 'tau_winf': (0.0273, 0.01, 0.07), 'w_star': (0.78, 0.5, 0.94)}

def smooth_step(values):
    return jax.nn.sigmoid(SHARPNESS * values)

def cell_constants(tissue):
    endo_cell = tissue == 1
    middle_cell = tissue == 2
    table = {}
    for label, column in TYPE_TABLE.items():
        table[label] = jnp.where(endo_cell, column[0], jnp.where(middle_cell, column[1], column[2])).astype(jnp.float32)
    return table

def collide(distributions, gate_states, tissue, stim_site, stim_amp):
    voltage = lax.optimization_barrier(jnp.sum(distributions, axis=0))
    const = cell_constants(tissue)
    slow_v = gate_states[0]
    slow_w = gate_states[1]
    slow_s = gate_states[2]
    step_v = smooth_step(voltage - 0.3)
    step_w = smooth_step(voltage - 0.13)
    step_minus = smooth_step(voltage - const['theta_vminus'])
    step_zero = smooth_step(voltage - const['theta_zero'])
    time_vminus = (1.0 - step_minus) * const['tau_v1minus'] + step_minus * const['tau_v2minus']
    time_wminus = const['tau_w1minus'] + (const['tau_w2minus'] - const['tau_w1minus']) * (1.0 + jnp.tanh(const['k_wminus'] * (voltage - const['u_wminus']))) * 0.5
    time_so = const['tau_so1'] + (const['tau_so2'] - const['tau_so1']) * (1.0 + jnp.tanh(const['k_so'] * (voltage - const['u_so']))) * 0.5
    time_s = (1.0 - step_w) * 2.7342 + step_w * const['tau_s2']
    time_o = (1.0 - step_zero) * const['tau_o1'] + step_zero * const['tau_o2']
    w_target = (1.0 - step_zero) * (1.0 - voltage / const['tau_winf']) + step_zero * const['w_star']
    fast_current = -slow_v * step_v * (voltage - 0.3) * (const['u_upper'] - voltage) / const['tau_fast']
    outward_current = voltage * (1.0 - step_w) / time_o + step_w / time_so
    slow_current = -step_w * slow_w * slow_s / const['tau_slow']
    stimulus = jnp.zeros_like(voltage)
    for site_index in range(stim_amp.shape[0]):
        stimulus = stimulus + jnp.where(stim_site == site_index + 1, stim_amp[site_index], 0.0)
    react = stimulus - (fast_current + outward_current + slow_current)
    change_v = (1.0 - step_v) * (1.0 - step_minus - slow_v) / time_vminus - step_v * slow_v / 1.4506
    change_w = (1.0 - step_w) * (w_target - slow_w) / time_wminus - step_w * slow_w / const['tau_wplus']
    change_s = ((1.0 + jnp.tanh(2.0994 * (voltage - 0.9087))) * 0.5 - slow_s) / time_s
    live = tissue > 0
    next_states = jnp.where(live, gate_states + STEP_TIME * jnp.stack([change_v, change_w, change_s]), gate_states)
    shape = (-1,) + (1,) * (distributions.ndim - 1)
    weights = jnp.array(LATTICE_WEIGHTS, dtype=distributions.dtype).reshape(shape)
    collided = distributions - (distributions - weights * voltage) / const['relax_time'] + STEP_TIME * weights * react
    collided = jnp.where(live, collided, 0.0)
    return (collided, next_states)

def shifted(extended, step_x, step_y, step_z):
    count_x = extended.shape[-3] - 2
    count_y = extended.shape[-2] - 2
    window = extended[..., 1 + step_x:1 + step_x + count_x, 1 + step_y:1 + step_y + count_y, :]
    if step_z == 1:
        window = jnp.concatenate([window[..., 1:], jnp.zeros_like(window[..., :1])], axis=-1)
    elif step_z == -1:
        window = jnp.concatenate([jnp.zeros_like(window[..., :1]), window[..., :-1]], axis=-1)
    return window

def propagate(extended, tissue_ext, tissue):
    moved = []
    for direction in range(7):
        vel_x, vel_y, vel_z = VELOCITIES[direction]
        source = shifted(extended[direction], -vel_x, -vel_y, -vel_z)
        source_live = shifted(tissue_ext, -vel_x, -vel_y, -vel_z)
        bounced = shifted(extended[OPPOSITE[direction]], 0, 0, 0)
        moved.append(jnp.where(source_live > 0, source, bounced))
    return jnp.where(tissue > 0, jnp.stack(moved), 0.0)

def lower_factor(gram):
    order = gram.shape[0]
    places = lax.broadcasted_iota(jnp.int32, (order,), 0)
    lower = jnp.zeros_like(gram)
    for column_index in range(order):
        column = gram[:, column_index] - jnp.dot(lower, lower[column_index], precision=lax.Precision.HIGHEST)
        pivot = jnp.sqrt(column[column_index])
        filled = jnp.where(places > column_index, column / pivot, jnp.where(places == column_index, pivot, 0.0))
        lower = lower + filled[:, None] * (places == column_index).astype(gram.dtype)[None, :]
    return lower

def lower_inverse(lower):
    order = lower.shape[0]
    places = lax.broadcasted_iota(jnp.int32, (order,), 0)
    inverse = jnp.zeros_like(lower)
    for row_index in range(order):
        unit = (places == row_index).astype(lower.dtype)
        row = (unit - jnp.dot(lower[row_index], inverse, precision=lax.Precision.HIGHEST)) / lower[row_index, row_index]
        inverse = inverse + unit[:, None] * row[None, :]
    return inverse

def cholesky_qr(columns):
    gram = jnp.dot(columns, columns.T, precision=lax.Precision.HIGHEST)
    first = lower_factor(gram)
    whitened = jnp.dot(lower_inverse(first), columns, precision=lax.Precision.HIGHEST)
    second = lower_factor(jnp.dot(whitened, whitened.T, precision=lax.Precision.HIGHEST))
    return jnp.dot(second.T, first.T, precision=lax.Precision.HIGHEST)

def recorded(history, voltages, record_column):
    places = lax.broadcasted_iota(jnp.int32, (history.shape[0], 1, 1, 1), 0)
    snapshots = history
    for step_index in range(len(voltages)):
        snapshots = jnp.where(places == record_column[step_index], voltages[step_index][None], snapshots)
    return snapshots

def reference(distributions, gate_states, history, tissue, stim_site, stim_amp, record_column):
    tissue_ext = jnp.pad(tissue, ((1, 1), (1, 1), (0, 0)))
    voltages = []
    for lattice_step in range(STEPS):
        collided, gate_states = collide(distributions, gate_states, tissue, stim_site, stim_amp)
        extended = jnp.pad(collided, ((0, 0), (1, 1), (1, 1), (0, 0)))
        distributions = propagate(extended, tissue_ext, tissue)
        voltages.append(lax.optimization_barrier(jnp.sum(distributions, axis=0)))
    snapshots = recorded(history, voltages, record_column)
    columns = snapshots.reshape(snapshots.shape[0], -1)
    upper = cholesky_qr(columns)
    inverse = lower_inverse(upper.T).T
    basis_rows = jnp.dot(inverse.T, columns, precision=lax.Precision.HIGHEST)
    scale = math.sqrt(NX * NY * NZ)
    return (distributions, gate_states, (basis_rows * scale).reshape(snapshots.shape), upper / scale)
```

```python
import functools
import math

import jax
import jax.numpy as jnp
from jax import lax
from jax.experimental import pallas as pl
from jax.experimental.pallas import tpu as pltpu
from jax.sharding import PartitionSpec as P

MESH = pl.DeviceIdType.MESH
DT = 0.1
DEAD = -1e30
LIMIT = -1e29
F32 = jnp.float32
BF16 = jnp.bfloat16
NT = (((1,), (1,)), ((), ()))
GROUP = 16


def split_rows(a, shape):
    lead = a.shape[:-2]
    a = jnp.swapaxes(a.reshape(lead + (4, 2, 128)), -3, -2)
    return a.reshape(shape)


def join_rows(a, shape):
    lead = shape[:-2]
    a = jnp.swapaxes(a.reshape(lead + (2, 4, 128)), -3, -2)
    return a.reshape(shape)


def typed(tissue):
    endo = tissue == 1
    mid = tissue == 2

    def pick(a, b, c):
        if a == b == c:
            return a
        if b == c:
            return jnp.where(endo, F32(a), F32(c))
        if a == c:
            return jnp.where(mid, F32(b), F32(c))
        if a == b:
            return jnp.where(tissue == 1, F32(a), jnp.where(mid, F32(a), F32(c)))
        return jnp.where(endo, F32(a), jnp.where(mid, F32(b), F32(c)))

    return pick


def each(fn, *columns):
    return tuple(fn(*entry) for entry in zip(*columns))


def collide(f, v, w, s, tissue, stim):
    pick = typed(tissue)
    live = tissue > 0
    u = ((f[0] + f[1]) + (f[2] + f[3])) + ((f[4] + f[5]) + f[6])
    hv = 0.5 + 0.5 * jnp.tanh(25.0 * (u - 0.3))
    hw = 0.5 + 0.5 * jnp.tanh(25.0 * (u - 0.13))
    hm = 0.5 + 0.5 * jnp.tanh(25.0 * (u - pick(0.2, 0.1, 0.006)))
    ho = 0.5 + 0.5 * jnp.tanh(25.0 * (u - pick(0.006, 0.005, 0.006)))
    nv, nw, no = 1.0 - hv, 1.0 - hw, 1.0 - ho
    tv1, tv2 = (75.0, 80.0, 60.0), (10.0, 1.4506, 1150.0)
    tvm = pick(*tv1) + hm * pick(*each(lambda a, b: b - a, tv1, tv2))
    tw1, tw2 = (6.0, 70.0, 60.0), (140.0, 8.0, 15.0)
    thw = jnp.tanh(pick(200.0, 200.0, 65.0) * (u - pick(0.016, 0.016, 0.03)))
    twm = pick(*each(lambda a, b: (a + b) / 2, tw1, tw2)) + thw * pick(
        *each(lambda a, b: (b - a) / 2, tw1, tw2)
    )
    ts1, ts2 = (40.0, 91.0, 30.0181), (1.2, 0.8, 0.9957)
    tht = jnp.tanh(pick(2.0, 2.1, 2.0458) * (u - pick(0.65, 0.6, 0.65)))
    tso = pick(*each(lambda a, b: (a + b) / 2, ts1, ts2)) + tht * pick(
        *each(lambda a, b: (b - a) / 2, ts1, ts2)
    )
    ts = 2.7342 + hw * pick(*each(lambda a: a - 2.7342, (2.0, 4.0, 16.0)))
    to1, to2 = (470.0, 410.0, 400.0), (6.0, 7.0, 6.0)
    to = pick(*to1) + ho * pick(*each(lambda a, b: b - a, to1, to2))
    winf = no * (1.0 - u * pick(*each(lambda a: 1 / a, (0.0273, 0.01, 0.07)))) + ho * pick(
        0.78, 0.5, 0.94
    )
    minus_fi = v * hv * (u - 0.3) * (pick(1.56, 1.61, 1.55) - u) * pick(
        *each(lambda a: 1 / a, (0.1, 0.078, 0.11))
    )
    outward = u * nw / to + hw / tso
    minus_si = hw * w * s * pick(*each(lambda a: 1 / a, (2.9013, 3.3849, 1.8875)))
    react = stim + minus_fi - outward + minus_si
    dv = nv * (1.0 - hm - v) / tvm - hv * v * (1 / 1.4506)
    dw = nw * (winf - w) / twm - hw * w * pick(*each(lambda a: 1 / a, (280.0, 280.0, 200.0)))
    ds = ((0.5 + 0.5 * jnp.tanh(2.0994 * (u - 0.9087))) - s) / ts
    gates = (
        jnp.where(live, v + DT * dv, v),
        jnp.where(live, w + DT * dw, w),
        jnp.where(live, s + DT * ds, s),
    )
    rate = pick(*each(lambda a: 1 / a, (0.95, 0.8, 1.1)))
    keep = pick(*each(lambda a: 1 - 1 / a, (0.95, 0.8, 1.1)))
    share = 0.125 * (u * rate + DT * react)
    g = [jnp.where(live, f[0] * keep + 2.0 * share, DEAD)]
    for i in range(1, 7):
        g.append(jnp.where(live, f[i] * keep + share, DEAD))
    return g, gates


def kernel(
    f_hbm, g_hbm, x_hbm, t_hbm, s_hbm, amp, rc,
    fo_hbm, go_hbm, y_hbm, zt_ref, up_ref,
    fv, gv, xv, tv, sv, stim, cc, cxp, cxm, ysp, ysm, yrp, yrm, u1, u2, yv, red,
    load_sem, out_sem, hs_sem, hr_sem, as_sem, ar_sem,
):
    planes = fv.shape[1]
    quads = planes // 4
    slabs, tiles = lax.axis_size("slab"), lax.axis_size("tile")
    slab, tile = lax.axis_index("slab"), lax.axis_index("tile")
    core, yy, zz = lax.rem(tile, 2), lax.rem(tile // 2, 4), tile // 8

    loads = [
        pltpu.make_async_copy(src, dst, load_sem.at[i])
        for i, (src, dst) in enumerate(
            ((f_hbm, fv), (t_hbm, tv), (s_hbm, sv), (g_hbm, gv), (x_hbm, xv))
        )
    ]
    for copy in loads:
        copy.start()

    right = (lax.rem(slab + 1, slabs), tile)
    left = (lax.rem(slab + slabs - 1, slabs), tile)
    up = (slab, lax.rem(tile + 1, tiles))
    down = (slab, lax.rem(tile + tiles - 1, tiles))
    rank = (slab * 4 + yy, zz * 2 + core)

    def partner(stage, k):
        other = lax.rem(rank[stage] + k, GROUP)
        if stage == 0:
            return (other // 4, zz * 8 + lax.rem(other, 4) * 2 + core)
        return (slab, other // 2 * 8 + yy * 2 + lax.rem(other, 2))

    barrier = pltpu.get_barrier_semaphore()
    for dev in (right, left, up, down):
        pl.semaphore_signal(barrier, inc=1, device_id=dev, device_id_type=MESH)
    for stage in range(2):

        def greet(k, carry, stage=stage):
            pl.semaphore_signal(barrier, inc=1, device_id=partner(stage, k), device_id_type=MESH)
            return carry

        lax.fori_loop(1, GROUP, greet, 0)

    row4 = lax.broadcasted_iota(jnp.int32, (8, 128), 0)
    lane = lax.broadcasted_iota(jnp.int32, (4, 8, 128), 2)
    row = lax.broadcasted_iota(jnp.int32, (4, 8, 128), 1)
    yrow = lax.rem(row, 4)
    yrow2 = lax.rem(row4, 4)

    def store_collided(step, q, g):
        p = pl.ds(q * 4, 4)
        cc[0, p] = g[0]
        cc[1, p] = g[3]
        cc[2, p] = g[4]
        cc[3, p] = g[5]
        cc[4, p] = g[6]
        cxp[step, pl.ds(q * 4 + 1, 4)] = g[1]
        cxm[step, p] = g[2]
        face_p = g[3][3]
        face_m = g[4][0]
        for k in range(3):
            face_p = jnp.where(yrow2 == k, pltpu.roll(g[3][k], 5 + k, 0), face_p)
        for k in range(1, 4):
            face_m = jnp.where(yrow2 == k, pltpu.roll(g[4][k], k, 0), face_m)
        ysp[step, q] = face_p
        ysm[step, q] = face_m

    def halos(step):
        pairs = (
            (cxp.at[step, pl.ds(planes, 1)], cxp.at[step, pl.ds(0, 1)], right),
            (cxm.at[step, pl.ds(0, 1)], cxm.at[step, pl.ds(planes, 1)], left),
            (ysp.at[step], yrp.at[step], up),
            (ysm.at[step], yrm.at[step], down),
        )
        return [
            pltpu.make_async_remote_copy(
                src_ref=src,
                dst_ref=dst,
                send_sem=hs_sem.at[step * 4 + i],
                recv_sem=hr_sem.at[step * 4 + i],
                device_id=dev,
                device_id_type=MESH,
            )
            for i, (src, dst, dev) in enumerate(pairs)
        ]

    def settle_halos(step):
        for copy in halos(step):
            copy.wait_recv()
        cxp[step, pl.ds(0, 1)] = jnp.where(slab == 0, DEAD, cxp[step, pl.ds(0, 1)])
        cxm[step, pl.ds(planes, 1)] = jnp.where(
            slab == slabs - 1, DEAD, cxm[step, pl.ds(planes, 1)]
        )
        yrp[step] = jnp.where(tile == 0, DEAD, yrp[step])
        yrm[step] = jnp.where(tile == tiles - 1, DEAD, yrm[step])

    def propagate(step, q, tissue):
        p = pl.ds(q * 4, 4)
        p1 = pl.ds(q * 4 + 1, 4)

        def bounce(moved, back):
            return jnp.where(moved > LIMIT, moved, back)

        gx1, gx2 = cxp[step, p1], cxm[step, p]
        gy1, gy2, gz1, gz2 = cc[1, p], cc[2, p], cc[3, p], cc[4, p]
        hp, hm = yrp[step, q], yrm[step, q]
        halo_p = jnp.stack([hp] + [pltpu.roll(hp, 8 - k, 0) for k in range(1, 4)])
        halo_m = jnp.stack([pltpu.roll(hm, 3 - k, 0) for k in range(3)] + [hm])
        my1 = jnp.where(yrow == 0, halo_p, pltpu.roll(gy1, 1, 1))
        my2 = jnp.where(yrow == 3, halo_m, pltpu.roll(gy2, 7, 1))
        rz1 = pltpu.roll(gz1, 1, 2)
        rz2 = pltpu.roll(gz2, 127, 2)
        mz1 = jnp.where(lane == 0, jnp.where(row >= 4, pltpu.roll(rz1, 4, 1), DEAD), rz1)
        mz2 = jnp.where(lane == 127, jnp.where(row < 4, pltpu.roll(rz2, 4, 1), DEAD), rz2)
        f = (
            cc[0, p],
            bounce(cxp[step, p], gx2),
            bounce(cxm[step, p1], gx1),
            bounce(my1, gy2),
            bounce(my2, gy1),
            bounce(mz1, gz2),
            bounce(mz2, gz1),
        )
        live = tissue > 0
        f = [jnp.where(live, part, 0.0) for part in f]
        u = ((f[0] + f[1]) + (f[2] + f[3])) + ((f[4] + f[5]) + f[6])
        return f, u

    def advance(q, f, current):
        p = pl.ds(q * 4, 4)
        g, gates = collide(f, gv[0, p], gv[1, p], gv[2, p], tv[p], current)
        for i in range(3):
            gv[i, p] = gates[i]
        return g

    def reduce_copy(which, stage, k):
        at = (which * 2 + stage) * GROUP
        slot = red.at[at + rank[stage]]
        return pltpu.make_async_remote_copy(
            src_ref=slot,
            dst_ref=slot,
            send_sem=as_sem.at[at + k],
            recv_sem=ar_sem.at[at + k],
            device_id=partner(stage, k),
            device_id_type=MESH,
        )

    def reduce_send(which, stage, block):
        red[(which * 2 + stage) * GROUP + rank[stage]] = block

        def send(k, carry):
            reduce_copy(which, stage, k).start()
            return carry

        lax.fori_loop(1, GROUP, send, 0)

    def reduce_sum(which, stage):
        def take(k, carry):
            reduce_copy(which, stage, k).wait_recv()
            return carry

        lax.fori_loop(1, GROUP, take, 0)
        at = (which * 2 + stage) * GROUP
        parts = [red[at + i] for i in range(GROUP)]
        while len(parts) > 1:
            parts = [a + b for a, b in zip(parts[::2], parts[1::2])]
        return parts[0]

    def packed(m):
        return jnp.concatenate([m[8 * b : 8 * b + 8] for b in range(4)], axis=1)

    def unpacked(m):
        return jnp.concatenate([m[:, 32 * b : 32 * b + 32] for b in range(4)], axis=0)

    ri = lax.broadcasted_iota(jnp.int32, (32, 32), 0)
    ci = lax.broadcasted_iota(jnp.int32, (32, 32), 1)

    def eliminate(gram):
        m = jnp.concatenate([gram, jnp.where(ri == ci, 1.0, 0.0)], axis=1)
        below = lax.broadcasted_iota(jnp.int32, (32, 64), 0)
        for j in range(31):
            scaled = m[j : j + 1, :] / m[j : j + 1, j : j + 1]
            m = m - jnp.where(below > j, m[:, j : j + 1] * scaled, 0.0)
        upper = m[:, :32]
        pivot = jnp.sum(jnp.where(ri == ci, upper, 0.0), axis=1, keepdims=True)
        scale = 1.0 / jnp.sqrt(pivot)
        return jnp.where(ri <= ci, upper * scale, 0.0), m[:, 32:] * scale

    def thirds(a):
        hi = a.astype(BF16)
        rest = a - hi.astype(F32)
        mid = rest.astype(BF16)
        return hi, mid, (rest - mid.astype(F32)).astype(BF16)

    for copy in loads[:4]:
        copy.wait()

    def first(q, carry):
        p = pl.ds(q * 4, 4)
        site = sv[p]
        current = jnp.zeros((4, 8, 128), F32)
        for k in range(8):
            current = jnp.where(site == k + 1, amp[k], current)
        stim[p] = current
        store_collided(0, q, advance(q, [fv[i, p] for i in range(7)], current))
        return carry

    lax.fori_loop(0, quads, first, 0)
    pl.semaphore_wait(barrier, 4 + 2 * (GROUP - 1))
    for copy in halos(0):
        copy.start()

    loads[4].wait()
    rows = planes * 8

    def old_gram(x, acc):
        chunk = jnp.concatenate(
            [xv[pl.ds(x * 8 + r, 32, stride=rows), :] for r in range(8)], axis=1
        )
        hi = chunk.astype(BF16)
        lo = (chunk - hi.astype(F32)).astype(BF16)
        both = jnp.concatenate([hi, lo], axis=0)
        return acc + lax.dot_general(both, both, NT, preferred_element_type=F32)

    acc = lax.fori_loop(0, planes, old_gram, jnp.zeros((64, 64), F32))
    reduce_send(0, 0, packed(acc[:32, :32] + acc[:32, 32:] + acc[32:, :32] + acc[32:, 32:]))

    settle_halos(0)

    def second(q, carry):
        p = pl.ds(q * 4, 4)
        f, u = propagate(0, q, tv[p])
        u1[p] = u
        for i in range(7):
            fv[i, p] = f[i]
        return carry

    lax.fori_loop(0, quads, second, 0)

    def third(q, carry):
        p = pl.ds(q * 4, 4)
        store_collided(1, q, advance(q, [fv[i, p] for i in range(7)], stim[p]))
        return carry

    lax.fori_loop(0, quads, third, 0)
    for copy in halos(1):
        copy.start()
    reduce_send(0, 1, reduce_sum(0, 0))
    gates_out = pltpu.make_async_copy(gv, go_hbm, out_sem.at[0])
    gates_out.start()

    settle_halos(1)

    def fourth(q, carry):
        p = pl.ds(q * 4, 4)
        f, u = propagate(1, q, tv[p])
        u2[p] = u
        for i in range(7):
            fv[i, p] = f[i]
        return carry

    lax.fori_loop(0, quads, fourth, 0)
    f_out = pltpu.make_async_copy(fv, fo_hbm, out_sem.at[1])
    f_out.start()

    gram = unpacked(reduce_sum(0, 1))
    taken = (ri == rc[0]) | (ri == rc[1]) | (ci == rc[0]) | (ci == rc[1])
    gram = jnp.where(taken, jnp.where(ri == ci, 1.0, 0.0), gram)
    r0, t0 = eliminate(gram)
    th, tm, tl = thirds(t0)
    wide = jnp.concatenate([th, th, tm, th, tm, tl], axis=1)

    column = lax.broadcasted_iota(jnp.int32, (32, 128), 0)
    is1, is2 = column == rc[0], column == rc[1]

    def new_gram(x, acc):
        pieces = []
        for r in range(8):
            piece = xv[pl.ds(x * 8 + r, 32, stride=rows), :]
            piece = jnp.where(is1, u1[x, r : r + 1, :], piece)
            pieces.append(jnp.where(is2, u2[x, r : r + 1, :], piece))
        hi, mid, lo = thirds(jnp.concatenate(pieces, axis=1))
        tall = jnp.concatenate([hi, mid, hi, lo, mid, hi], axis=0)
        y = jnp.dot(wide, tall, preferred_element_type=F32)
        for r in range(8):
            yv[x * 8 + r] = y[:, 128 * r : 128 * r + 128]
        parts = jnp.concatenate(thirds(y), axis=0)
        return acc + lax.dot_general(parts, parts, NT, preferred_element_type=F32)

    acc = lax.fori_loop(0, planes, new_gram, jnp.zeros((96, 96), F32))
    a, b, c = (acc[32 * i : 32 * i + 32] for i in range(3))
    gram = a[:, :32] + ((a[:, 32:64] + b[:, :32]) + (b[:, 32:64] + (a[:, 64:] + c[:, :32])))
    reduce_send(1, 0, packed(gram))
    y_out = pltpu.make_async_copy(yv, y_hbm, out_sem.at[2])
    y_out.start()
    reduce_send(1, 1, reduce_sum(1, 0))
    r2, z2 = eliminate(unpacked(reduce_sum(1, 1)))
    norm = math.sqrt(planes * 1024 * slabs * tiles)
    zt_ref[...] = z2 * norm
    up_ref[...] = jnp.dot(
        r2, r0, precision=lax.Precision.HIGHEST, preferred_element_type=F32
    ) * (1.0 / norm)

    gates_out.wait()
    f_out.wait()
    y_out.wait()
    for step in range(2):
        for copy in halos(step):
            copy.wait_send()
    for which in range(2):
        for stage in range(2):

            def sent(k, carry, which=which, stage=stage):
                reduce_copy(which, stage, k).wait_send()
                return carry

            lax.fori_loop(1, GROUP, sent, 0)


def basis_kernel(y_ref, f_ref, g_ref, z_ref, r_ref, q_ref, fo_ref, go_ref, ro_ref):
    z = z_ref[...]
    zh = z.astype(BF16)
    zl = (z - zh.astype(F32)).astype(BF16)
    wide = jnp.concatenate([zh, zh, zl], axis=1)
    for x in range(y_ref.shape[0] // 8):
        chunk = jnp.concatenate([y_ref[x * 8 + r] for r in range(8)], axis=1)
        hi = chunk.astype(BF16)
        lo = (chunk - hi.astype(F32)).astype(BF16)
        q = jnp.dot(wide, jnp.concatenate([hi, lo, hi], axis=0), preferred_element_type=F32)
        for r in range(8):
            q_ref[:, x * 8 + r, :] = q[:, 128 * r : 128 * r + 128]
    fo_ref[...] = f_ref[...]
    go_ref[...] = g_ref[...]
    ro_ref[...] = r_ref[...]


def local(distributions, gate_states, history, tissue, stim_site, stim_amp, record_column):
    planes = distributions.shape[1]
    rows = planes * 8
    any_space = pl.BlockSpec(memory_space=pl.ANY)
    smem = pl.BlockSpec(memory_space=pltpu.SMEM)
    vmem = pl.BlockSpec(memory_space=pltpu.VMEM)
    grid_f = (7, planes, 8, 128)
    shapes = [
        jax.ShapeDtypeStruct(grid_f, F32),
        jax.ShapeDtypeStruct((3, planes, 8, 128), F32),
        jax.ShapeDtypeStruct((rows, 32, 128), F32),
        jax.ShapeDtypeStruct((32, 32), F32),
        jax.ShapeDtypeStruct((32, 32), F32),
    ]
    plane = (planes, 8, 128)
    scratch = [
        pltpu.VMEM(grid_f, F32),
        pltpu.VMEM((3,) + plane, F32),
        pltpu.VMEM((32 * rows, 128), F32),
        pltpu.VMEM(plane, jnp.int32),
        pltpu.VMEM(plane, jnp.int32),
        pltpu.VMEM(plane, F32),
        pltpu.VMEM((5,) + plane, F32),
        pltpu.VMEM((2, planes + 1, 8, 128), F32),
        pltpu.VMEM((2, planes + 1, 8, 128), F32),
        pltpu.VMEM((2, planes // 4, 8, 128), F32),
        pltpu.VMEM((2, planes // 4, 8, 128), F32),
        pltpu.VMEM((2, planes // 4, 8, 128), F32),
        pltpu.VMEM((2, planes // 4, 8, 128), F32),
        pltpu.VMEM(plane, F32),
        pltpu.VMEM(plane, F32),
        pltpu.VMEM((rows, 32, 128), F32),
        pltpu.VMEM((4 * GROUP, 8, 128), F32),
        pltpu.SemaphoreType.DMA((5,)),
        pltpu.SemaphoreType.DMA((3,)),
        pltpu.SemaphoreType.DMA((8,)),
        pltpu.SemaphoreType.DMA((8,)),
        pltpu.SemaphoreType.DMA((4 * GROUP,)),
        pltpu.SemaphoreType.DMA((4 * GROUP,)),
    ]
    f, g, y, zt, up = pl.pallas_call(
        kernel,
        out_shape=shapes,
        in_specs=[any_space] * 5 + [smem] * 2,
        out_specs=[any_space] * 3 + [vmem] * 2,
        scratch_shapes=scratch,
        compiler_params=pltpu.CompilerParams(
            collective_id=0, has_side_effects=True, vmem_limit_bytes=58 << 20
        ),
    )(
        split_rows(distributions, grid_f),
        split_rows(gate_states, (3,) + plane),
        split_rows(history, (32 * rows, 128)),
        split_rows(tissue, plane),
        split_rows(stim_site, plane),
        stim_amp,
        record_column,
    )
    part = 32
    q, f, g, up = pl.pallas_call(
        basis_kernel,
        grid=(rows // part,),
        out_shape=[
            jax.ShapeDtypeStruct((32, rows, 128), F32),
            jax.ShapeDtypeStruct((7, rows, 128), F32),
            jax.ShapeDtypeStruct((3, rows, 128), F32),
            jax.ShapeDtypeStruct((32, 32), F32),
        ],
        in_specs=[
            pl.BlockSpec((part, 32, 128), lambda i: (i, 0, 0)),
            pl.BlockSpec((7, part, 128), lambda i: (0, i, 0)),
            pl.BlockSpec((3, part, 128), lambda i: (0, i, 0)),
            pl.BlockSpec((32, 32), lambda i: (0, 0)),
            pl.BlockSpec((32, 32), lambda i: (0, 0)),
        ],
        out_specs=[
            pl.BlockSpec((32, part, 128), lambda i: (0, i, 0)),
            pl.BlockSpec((7, part, 128), lambda i: (0, i, 0)),
            pl.BlockSpec((3, part, 128), lambda i: (0, i, 0)),
            pl.BlockSpec((32, 32), lambda i: (0, 0)),
        ],
        compiler_params=pltpu.CompilerParams(vmem_limit_bytes=58 << 20),
    )(y, f.reshape(7, rows, 128), g.reshape(3, rows, 128), zt, up)
    return (
        join_rows(f, distributions.shape),
        join_rows(g, gate_states.shape),
        join_rows(q, history.shape),
        up,
    )


def solution(mesh):
    field = P(None, "slab", "tile", None)
    label = P("slab", "tile", None)
    return jax.shard_map(
        local,
        mesh=mesh,
        in_specs=(field, field, field, label, label, P(), P()),
        out_specs=(field, field, field, P()),
        check_vma=False,
    )
```

```python
import functools
import math

import jax
import jax.numpy as jnp
from jax import lax
from jax.experimental import pallas as pl
from jax.experimental.pallas import tpu as pltpu
from jax.sharding import PartitionSpec as P

MESH = pl.DeviceIdType.MESH
DT = 0.1
DEAD = -1e30
LIMIT = -1e29
F32 = jnp.float32
BF16 = jnp.bfloat16
NT = (((1,), (1,)), ((), ()))
GROUP = 16
PANEL = 4


def split_rows(a, shape):
    lead = a.shape[:-2]
    a = jnp.swapaxes(a.reshape(lead + (4, 2, 128)), -3, -2)
    return a.reshape(shape)


def join_rows(a, shape):
    lead = shape[:-2]
    a = jnp.swapaxes(a.reshape(lead + (2, 4, 128)), -3, -2)
    return a.reshape(shape)


def typed(tissue):
    endo = tissue == 1
    mid = tissue == 2

    def pick(a, b, c):
        if a == b == c:
            return a
        if b == c:
            return jnp.where(endo, F32(a), F32(c))
        if a == c:
            return jnp.where(mid, F32(b), F32(c))
        if a == b:
            return jnp.where(tissue == 1, F32(a), jnp.where(mid, F32(a), F32(c)))
        return jnp.where(endo, F32(a), jnp.where(mid, F32(b), F32(c)))

    return pick


def each(fn, *columns):
    return tuple(fn(*entry) for entry in zip(*columns))


def collide(f, v, w, s, tissue, stim):
    pick = typed(tissue)
    live = tissue > 0
    u = ((f[0] + f[1]) + (f[2] + f[3])) + ((f[4] + f[5]) + f[6])
    hv = 0.5 + 0.5 * jnp.tanh(25.0 * (u - 0.3))
    hw = 0.5 + 0.5 * jnp.tanh(25.0 * (u - 0.13))
    hm = 0.5 + 0.5 * jnp.tanh(25.0 * (u - pick(0.2, 0.1, 0.006)))
    ho = 0.5 + 0.5 * jnp.tanh(25.0 * (u - pick(0.006, 0.005, 0.006)))
    nv, nw, no = 1.0 - hv, 1.0 - hw, 1.0 - ho
    tv1, tv2 = (75.0, 80.0, 60.0), (10.0, 1.4506, 1150.0)
    tvm = pick(*tv1) + hm * pick(*each(lambda a, b: b - a, tv1, tv2))
    tw1, tw2 = (6.0, 70.0, 60.0), (140.0, 8.0, 15.0)
    thw = jnp.tanh(pick(200.0, 200.0, 65.0) * (u - pick(0.016, 0.016, 0.03)))
    twm = pick(*each(lambda a, b: (a + b) / 2, tw1, tw2)) + thw * pick(
        *each(lambda a, b: (b - a) / 2, tw1, tw2)
    )
    ts1, ts2 = (40.0, 91.0, 30.0181), (1.2, 0.8, 0.9957)
    tht = jnp.tanh(pick(2.0, 2.1, 2.0458) * (u - pick(0.65, 0.6, 0.65)))
    tso = pick(*each(lambda a, b: (a + b) / 2, ts1, ts2)) + tht * pick(
        *each(lambda a, b: (b - a) / 2, ts1, ts2)
    )
    ts = 2.7342 + hw * pick(*each(lambda a: a - 2.7342, (2.0, 4.0, 16.0)))
    to1, to2 = (470.0, 410.0, 400.0), (6.0, 7.0, 6.0)
    to = pick(*to1) + ho * pick(*each(lambda a, b: b - a, to1, to2))
    winf = no * (1.0 - u * pick(*each(lambda a: 1 / a, (0.0273, 0.01, 0.07)))) + ho * pick(
        0.78, 0.5, 0.94
    )
    minus_fi = v * hv * (u - 0.3) * (pick(1.56, 1.61, 1.55) - u) * pick(
        *each(lambda a: 1 / a, (0.1, 0.078, 0.11))
    )
    outward = u * nw / to + hw / tso
    minus_si = hw * w * s * pick(*each(lambda a: 1 / a, (2.9013, 3.3849, 1.8875)))
    react = stim + minus_fi - outward + minus_si
    dv = nv * (1.0 - hm - v) / tvm - hv * v * (1 / 1.4506)
    dw = nw * (winf - w) / twm - hw * w * pick(*each(lambda a: 1 / a, (280.0, 280.0, 200.0)))
    ds = ((0.5 + 0.5 * jnp.tanh(2.0994 * (u - 0.9087))) - s) / ts
    gates = (
        jnp.where(live, v + DT * dv, v),
        jnp.where(live, w + DT * dw, w),
        jnp.where(live, s + DT * ds, s),
    )
    rate = pick(*each(lambda a: 1 / a, (0.95, 0.8, 1.1)))
    keep = pick(*each(lambda a: 1 - 1 / a, (0.95, 0.8, 1.1)))
    share = 0.125 * (u * rate + DT * react)
    g = [jnp.where(live, f[0] * keep + 2.0 * share, DEAD)]
    for i in range(1, 7):
        g.append(jnp.where(live, f[i] * keep + share, DEAD))
    return g, gates


def kernel(
    f_hbm, g_hbm, x_hbm, t_hbm, s_hbm, amp, rc,
    f_out, g_out, y_out, zt_ref, up_ref,
    fv, gv, xv, tv, sv, stim, cc, cxp, cxm, ysp, ysm, yrp, yrm, u1, u2,
    xs, acc1, acc2, red,
    load_sem, hs_sem, hr_sem, as_sem, ar_sem,
):
    planes = fv.shape[1]
    quads = planes // 4
    slabs, tiles = lax.axis_size("slab"), lax.axis_size("tile")
    slab, tile = lax.axis_index("slab"), lax.axis_index("tile")
    core, yy, zz = lax.rem(tile, 2), lax.rem(tile // 2, 4), tile // 8

    loads = [
        pltpu.make_async_copy(src, dst, load_sem.at[i])
        for i, (src, dst) in enumerate(
            ((x_hbm, xv), (f_hbm, fv), (t_hbm, tv), (s_hbm, sv), (g_hbm, gv))
        )
    ]
    for copy in loads:
        copy.start()

    right = (lax.rem(slab + 1, slabs), tile)
    left = (lax.rem(slab + slabs - 1, slabs), tile)
    up = (slab, lax.rem(tile + 1, tiles))
    down = (slab, lax.rem(tile + tiles - 1, tiles))
    rank = (slab * 4 + yy, zz * 2 + core)

    def partner(stage, k):
        other = lax.rem(rank[stage] + k, GROUP)
        if stage == 0:
            return (other // 4, zz * 8 + lax.rem(other, 4) * 2 + core)
        return (slab, other // 2 * 8 + yy * 2 + lax.rem(other, 2))

    barrier = pltpu.get_barrier_semaphore()
    for dev in (right, left, up, down):
        pl.semaphore_signal(barrier, inc=1, device_id=dev, device_id_type=MESH)
    for stage in range(2):

        def greet(k, carry, stage=stage):
            pl.semaphore_signal(barrier, inc=1, device_id=partner(stage, k), device_id_type=MESH)
            return carry

        lax.fori_loop(1, GROUP, greet, 0)

    row4 = lax.broadcasted_iota(jnp.int32, (8, 128), 0)
    lane = lax.broadcasted_iota(jnp.int32, (4, 8, 128), 2)
    row = lax.broadcasted_iota(jnp.int32, (4, 8, 128), 1)
    yrow = lax.rem(row, 4)
    yrow2 = lax.rem(row4, 4)

    def store_collided(step, q, g):
        p = pl.ds(q * 4, 4)
        cc[0, p] = g[0]
        cc[1, p] = g[3]
        cc[2, p] = g[4]
        cc[3, p] = g[5]
        cc[4, p] = g[6]
        cxp[step, pl.ds(q * 4 + 1, 4)] = g[1]
        cxm[step, p] = g[2]
        face_p = g[3][3]
        face_m = g[4][0]
        for k in range(3):
            face_p = jnp.where(yrow2 == k, pltpu.roll(g[3][k], 5 + k, 0), face_p)
        for k in range(1, 4):
            face_m = jnp.where(yrow2 == k, pltpu.roll(g[4][k], k, 0), face_m)
        ysp[step, q] = face_p
        ysm[step, q] = face_m

    def halos(step):
        pairs = (
            (cxp.at[step, pl.ds(planes, 1)], cxp.at[step, pl.ds(0, 1)], right),
            (cxm.at[step, pl.ds(0, 1)], cxm.at[step, pl.ds(planes, 1)], left),
            (ysp.at[step], yrp.at[step], up),
            (ysm.at[step], yrm.at[step], down),
        )
        return [
            pltpu.make_async_remote_copy(
                src_ref=src,
                dst_ref=dst,
                send_sem=hs_sem.at[step * 4 + i],
                recv_sem=hr_sem.at[step * 4 + i],
                device_id=dev,
                device_id_type=MESH,
            )
            for i, (src, dst, dev) in enumerate(pairs)
        ]

    def settle_halos(step):
        for copy in halos(step):
            copy.wait_recv()
        cxp[step, pl.ds(0, 1)] = jnp.where(slab == 0, DEAD, cxp[step, pl.ds(0, 1)])
        cxm[step, pl.ds(planes, 1)] = jnp.where(
            slab == slabs - 1, DEAD, cxm[step, pl.ds(planes, 1)]
        )
        yrp[step] = jnp.where(tile == 0, DEAD, yrp[step])
        yrm[step] = jnp.where(tile == tiles - 1, DEAD, yrm[step])

    def propagate(step, q, tissue):
        p = pl.ds(q * 4, 4)
        p1 = pl.ds(q * 4 + 1, 4)

        def bounce(moved, back):
            return jnp.where(moved > LIMIT, moved, back)

        gx1, gx2 = cxp[step, p1], cxm[step, p]
        gy1, gy2, gz1, gz2 = cc[1, p], cc[2, p], cc[3, p], cc[4, p]
        hp, hm = yrp[step, q], yrm[step, q]
        halo_p = jnp.stack([hp] + [pltpu.roll(hp, 8 - k, 0) for k in range(1, 4)])
        halo_m = jnp.stack([pltpu.roll(hm, 3 - k, 0) for k in range(3)] + [hm])
        my1 = jnp.where(yrow == 0, halo_p, pltpu.roll(gy1, 1, 1))
        my2 = jnp.where(yrow == 3, halo_m, pltpu.roll(gy2, 7, 1))
        rz1 = pltpu.roll(gz1, 1, 2)
        rz2 = pltpu.roll(gz2, 127, 2)
        mz1 = jnp.where(lane == 0, jnp.where(row >= 4, pltpu.roll(rz1, 4, 1), DEAD), rz1)
        mz2 = jnp.where(lane == 127, jnp.where(row < 4, pltpu.roll(rz2, 4, 1), DEAD), rz2)
        f = (
            cc[0, p],
            bounce(cxp[step, p], gx2),
            bounce(cxm[step, p1], gx1),
            bounce(my1, gy2),
            bounce(my2, gy1),
            bounce(mz1, gz2),
            bounce(mz2, gz1),
        )
        live = tissue > 0
        f = [jnp.where(live, part, 0.0) for part in f]
        u = ((f[0] + f[1]) + (f[2] + f[3])) + ((f[4] + f[5]) + f[6])
        return f, u

    def advance(q, f, current, gates_to):
        p = pl.ds(q * 4, 4)
        g, gates = collide(f, gv[0, p], gv[1, p], gv[2, p], tv[p], current)
        for i in range(3):
            gates_to[i, p] = gates[i]
        return g

    def reduce_copy(which, stage, slot, k):
        return pltpu.make_async_remote_copy(
            src_ref=slot,
            dst_ref=slot,
            send_sem=as_sem.at[which * 2 + stage],
            recv_sem=ar_sem.at[which * 2 + stage],
            device_id=partner(stage, k),
            device_id_type=MESH,
        )

    def reduce_send(which, stage, block):
        at = (which * 2 + stage) * GROUP + rank[stage]
        red[at] = block
        for k in range(1, GROUP):
            reduce_copy(which, stage, red.at[at], k).start()

    def reduce_all(which, stage):
        return reduce_copy(
            which, stage, red.at[pl.ds((which * 2 + stage) * GROUP, GROUP - 1)], 1
        )

    def reduce_sum(which, stage):
        reduce_all(which, stage).wait_recv()
        at = (which * 2 + stage) * GROUP
        parts = [red[at + i] for i in range(GROUP)]
        while len(parts) > 1:
            parts = [a + b for a, b in zip(parts[::2], parts[1::2])]
        return parts[0]

    def packed(m):
        return jnp.concatenate([m[8 * b : 8 * b + 8] for b in range(4)], axis=1)

    def unpacked(m):
        return jnp.concatenate([m[:, 32 * b : 32 * b + 32] for b in range(4)], axis=0)

    ri = lax.broadcasted_iota(jnp.int32, (32, 32), 0)
    ci = lax.broadcasted_iota(jnp.int32, (32, 32), 1)

    eye = jnp.where(ri == ci, 1.0, 0.0)

    def eliminate(a):
        m = jnp.concatenate([a, eye], axis=1)
        below = lax.broadcasted_iota(jnp.int32, (32, 64), 0)
        for p in range(0, 32, PANEL):
            cols = [jnp.broadcast_to(m[:, p + k : p + k + 1], (32, 64)) for k in range(PANEL)]
            rows = [m[p + k : p + k + 1, :] for k in range(PANEL)]
            taken_off = 0.0
            for k in range(PANEL):
                j = p + k
                low = jnp.where(below > j, cols[k] * (1.0 / cols[k][j : j + 1, :]), 0.0)
                for q in range(k + 1, PANEL):
                    cols[q] = cols[q] - low * cols[q][j : j + 1, :]
                    rows[q] = rows[q] - low[p + q : p + q + 1, :] * rows[k]
                taken_off = taken_off + low * rows[k]
            m = m - taken_off
        upper = m[:, :32]
        pivot = jnp.sum(jnp.where(ri == ci, upper, 0.0), axis=1, keepdims=True)
        return jnp.where(ri <= ci, upper, 0.0), m[:, 32:], pivot

    wide_row = lax.broadcasted_iota(jnp.int32, (256, 256), 0)
    wide_col = lax.broadcasted_iota(jnp.int32, (256, 256), 1)
    same = lax.rem(wide_row, 8) == lax.rem(wide_col, 8)

    def folded(p):
        m = jnp.sum(jnp.where(same, p, 0.0).reshape(32, 8, 256), axis=1)
        place = lax.broadcasted_iota(jnp.int32, (256, 32), 0) // 8
        pick = jnp.where(place == lax.broadcasted_iota(jnp.int32, (256, 32), 1), 1.0, 0.0)
        return jnp.dot(m, pick, precision=lax.Precision.HIGHEST, preferred_element_type=F32)

    loads[0].wait()

    def pair(x):
        return jnp.concatenate([xv[:, 2 * x].reshape(256, 128), xv[:, 2 * x + 1].reshape(256, 128)], axis=1)

    acc1[...] = jnp.zeros((256, 256), F32)

    def old_gram(i, carry):
        parts = [pair(2 * i + k).astype(BF16) for k in range(2)]
        for k in range(2):
            xs[2 * i + k, :256] = parts[k]
        hi = jnp.concatenate(parts, axis=1)
        acc1[...] += lax.dot_general(hi, hi, NT, preferred_element_type=F32)
        return carry

    lax.fori_loop(0, quads, old_gram, 0)
    block = packed(folded(acc1[...]))
    pl.semaphore_wait(barrier, 4 + 2 * (GROUP - 1))
    reduce_send(0, 0, block)

    for copy in loads[1:]:
        copy.wait()

    def first(q, carry):
        p = pl.ds(q * 4, 4)
        site = sv[p]
        current = jnp.zeros((4, 8, 128), F32)
        for k in range(8):
            current = jnp.where(site == k + 1, amp[k], current)
        stim[p] = current
        store_collided(0, q, advance(q, [fv[i, p] for i in range(7)], current, gv))
        return carry

    lax.fori_loop(0, quads, first, 0)
    for copy in halos(0):
        copy.start()

    def finer(i, carry):
        rest = pair(i) - xs[i, :256].astype(F32)
        mid = rest.astype(BF16)
        xs[i, 256:512] = mid
        xs[i, 512:] = (rest - mid.astype(F32)).astype(BF16)
        return carry

    lax.fori_loop(0, planes // 2, finer, 0)

    reduce_send(0, 1, reduce_sum(0, 0))

    settle_halos(0)

    def second(q, carry):
        p = pl.ds(q * 4, 4)
        f, u = propagate(0, q, tv[p])
        u1[p] = u
        store_collided(1, q, advance(q, f, stim[p], g_out))
        return carry

    lax.fori_loop(0, quads, second, 0)
    for copy in halos(1):
        copy.start()

    gram = unpacked(reduce_sum(0, 1))
    taken = (ri == rc[0]) | (ri == rc[1]) | (ci == rc[0]) | (ci == rc[1])
    gram = jnp.where(taken, eye, gram * (1.0 + eye * 2.0**-16))
    _, inv0, pivot = eliminate(gram)
    t0 = (inv0 * (1.0 / jnp.sqrt(pivot))).astype(BF16)
    spread = spread_rows(t0)
    spread = jnp.concatenate([spread, spread, spread], axis=1)

    settle_halos(1)

    def fourth(q, carry):
        p = pl.ds(q * 4, 4)
        f, u = propagate(1, q, tv[p])
        u2[p] = u
        for i in range(7):
            f_out[i, p] = f[i]
        return carry

    lax.fori_loop(0, quads, fourth, 0)

    column = lax.broadcasted_iota(jnp.int32, (32, 8, 256), 0)
    is1, is2 = column == rc[0], column == rc[1]
    acc1[...] = jnp.zeros((256, 256), F32)
    acc2[...] = jnp.zeros((256, 256), F32)

    def whitened(i):
        y = jnp.dot(spread, xs[i], preferred_element_type=F32)
        new1 = jnp.concatenate([u1[2 * i], u1[2 * i + 1]], axis=1)
        new2 = jnp.concatenate([u2[2 * i], u2[2 * i + 1]], axis=1)
        y = jnp.where(is1, new1[None], jnp.where(is2, new2[None], y.reshape(32, 8, 256)))
        y = y.reshape(256, 256)
        hi = y.astype(BF16)
        lo = (y - hi.astype(F32)).astype(BF16)
        y_out[i, 0] = hi
        y_out[i, 1] = lo
        return hi, lo

    def new_gram(i, carry):
        (h1, l1), (h2, l2) = whitened(2 * i), whitened(2 * i + 1)
        every = jnp.concatenate([h1, h2, l1, l2], axis=1)
        acc1[...] += lax.dot_general(every, every, NT, preferred_element_type=F32)
        acc2[...] += lax.dot_general(
            every[:, :512], every[:, 512:], NT, preferred_element_type=F32
        )
        return carry

    lax.fori_loop(0, quads, new_gram, 0)
    cross = folded(acc2[...])
    gram = folded(acc1[...]) + (
        cross
        + lax.dot_general(
            eye, cross, NT, precision=lax.Precision.HIGHEST, preferred_element_type=F32
        )
    )
    reduce_send(1, 0, packed(gram))
    _, inv0, pivot = eliminate(t0.astype(F32))
    back = inv0 * (1.0 / pivot)
    reduce_send(1, 1, reduce_sum(1, 0))
    r2, inv2, pivot = eliminate(unpacked(reduce_sum(1, 1)))
    scale = 1.0 / jnp.sqrt(pivot)
    norm = math.sqrt(planes * 1024 * slabs * tiles)
    zt_ref[...] = inv2 * (scale * norm)
    up_ref[...] = lax.dot_general(
        r2 * scale, back, NT, precision=lax.Precision.HIGHEST, preferred_element_type=F32
    ) * (1.0 / norm)

    for step in range(2):
        for copy in halos(step):
            copy.wait_send()
    for which in range(2):
        for stage in range(2):
            reduce_all(which, stage).wait_send()


def spread_rows(t):
    place = lax.broadcasted_iota(jnp.int32, (256, 32), 0) // 8
    pick = jnp.where(place == lax.broadcasted_iota(jnp.int32, (256, 32), 1), 1.0, 0.0).astype(BF16)
    half = jnp.dot(pick, t, preferred_element_type=F32).astype(BF16)
    full = lax.dot_general(half, pick, NT, preferred_element_type=F32)
    row = lax.rem(lax.broadcasted_iota(jnp.int32, (256, 256), 0), 8)
    col = lax.rem(lax.broadcasted_iota(jnp.int32, (256, 256), 1), 8)
    return jnp.where(row == col, full, 0.0).astype(BF16)


def basis_kernel(
    y_ref, f_ref, g_ref, z_ref, r_ref, q_hbm, f_hbm, g_hbm, r_hbm, qv, q_sem, p_sem
):
    parts = q_sem.shape[0]
    pairs = y_ref.shape[0] // parts
    passed = [
        pltpu.make_async_copy(src, dst, p_sem.at[i])
        for i, (src, dst) in enumerate(((f_ref, f_hbm), (g_ref, g_hbm), (r_ref, r_hbm)))
    ]
    for copy in passed:
        copy.start()
    z = z_ref[...]
    hi = z.astype(BF16)
    spread = spread_rows(hi)
    rest = spread_rows((z - hi.astype(F32)).astype(BF16))
    wide = jnp.concatenate([spread, spread, rest], axis=1)
    stores = []
    for i in range(parts):
        for k in range(pairs):
            at = i * pairs + k
            tall = jnp.concatenate([y_ref[at, 0], y_ref[at, 1], y_ref[at, 0]], axis=0)
            q = jnp.dot(wide, tall, preferred_element_type=F32)
            for j in range(2):
                qv[:, 2 * at + j] = q[:, 128 * j : 128 * j + 128].reshape(32, 8, 128)
        planes = pl.ds(2 * i * pairs, 2 * pairs)
        stores.append(
            pltpu.make_async_copy(qv.at[:, planes], q_hbm.at[:, planes], q_sem.at[i])
        )
        stores[-1].start()
    for copy in passed + stores:
        copy.wait()


def local(distributions, gate_states, history, tissue, stim_site, stim_amp, record_column):
    planes = distributions.shape[1]
    hbm = pl.BlockSpec(memory_space=pltpu.HBM)
    any_space = pl.BlockSpec(memory_space=pl.ANY)
    smem = pl.BlockSpec(memory_space=pltpu.SMEM)
    vmem = pl.BlockSpec(memory_space=pltpu.VMEM)
    grid_f = (7, planes, 8, 128)
    shapes = [
        pltpu.VMEM(grid_f, F32),
        pltpu.VMEM((3, planes, 8, 128), F32),
        pltpu.VMEM((planes // 2, 2, 256, 256), BF16),
        pltpu.VMEM((32, 32), F32),
        pltpu.VMEM((32, 32), F32),
    ]
    plane = (planes, 8, 128)
    scratch = [
        pltpu.VMEM(grid_f, F32),
        pltpu.VMEM((3,) + plane, F32),
        pltpu.VMEM((32,) + plane, F32),
        pltpu.VMEM(plane, jnp.int32),
        pltpu.VMEM(plane, jnp.int32),
        pltpu.VMEM(plane, F32),
        pltpu.VMEM((5,) + plane, F32),
        pltpu.VMEM((2, planes + 1, 8, 128), F32),
        pltpu.VMEM((2, planes + 1, 8, 128), F32),
        pltpu.VMEM((2, planes // 4, 8, 128), F32),
        pltpu.VMEM((2, planes // 4, 8, 128), F32),
        pltpu.VMEM((2, planes // 4, 8, 128), F32),
        pltpu.VMEM((2, planes // 4, 8, 128), F32),
        pltpu.VMEM(plane, F32),
        pltpu.VMEM(plane, F32),
        pltpu.VMEM((planes // 2, 768, 256), BF16),
        pltpu.VMEM((256, 256), F32),
        pltpu.VMEM((256, 256), F32),
        pltpu.VMEM((4 * GROUP, 8, 128), F32),
        pltpu.SemaphoreType.DMA((5,)),
        pltpu.SemaphoreType.DMA((8,)),
        pltpu.SemaphoreType.DMA((8,)),
        pltpu.SemaphoreType.DMA((4,)),
        pltpu.SemaphoreType.DMA((4,)),
    ]
    f, g, y, zt, up = pl.pallas_call(
        kernel,
        out_shape=shapes,
        in_specs=[hbm] * 5 + [smem] * 2,
        out_specs=[vmem] * 5,
        scratch_shapes=scratch,
        compiler_params=pltpu.CompilerParams(
            collective_id=0, has_side_effects=True, vmem_limit_bytes=54 << 20
        ),
    )(
        split_rows(distributions, grid_f),
        split_rows(gate_states, (3,) + plane),
        split_rows(history, (32,) + plane),
        split_rows(tissue, plane),
        split_rows(stim_site, plane),
        stim_amp,
        record_column,
    )
    parts = 8
    q, f, g, up = pl.pallas_call(
        basis_kernel,
        out_shape=[
            jax.ShapeDtypeStruct((32,) + plane, F32),
            jax.ShapeDtypeStruct(grid_f, F32),
            jax.ShapeDtypeStruct((3,) + plane, F32),
            jax.ShapeDtypeStruct((32, 32), F32),
        ],
        in_specs=[vmem] * 5,
        out_specs=[any_space] * 4,
        scratch_shapes=[
            pltpu.VMEM((32,) + plane, F32),
            pltpu.SemaphoreType.DMA((parts,)),
            pltpu.SemaphoreType.DMA((3,)),
        ],
        compiler_params=pltpu.CompilerParams(vmem_limit_bytes=48 << 20),
    )(y, f, g, zt, up)
    return (
        join_rows(f, distributions.shape),
        join_rows(g, gate_states.shape),
        join_rows(q, history.shape),
        up,
    )


def solution(mesh):
    field = P(None, "slab", "tile", None)
    label = P("slab", "tile", None)
    return jax.shard_map(
        local,
        mesh=mesh,
        in_specs=(field, field, field, label, label, P(), P()),
        out_specs=(field, field, field, P()),
        check_vma=False,
    )
```

```python
import functools
import math

import jax
import jax.numpy as jnp
from jax import lax
from jax.experimental import pallas as pl
from jax.experimental.pallas import tpu as pltpu
from jax.sharding import PartitionSpec as P

MESH = pl.DeviceIdType.MESH
DT = 0.1
DEAD = -1e30
LIMIT = -1e29
F32 = jnp.float32
BF16 = jnp.bfloat16
NT = (((1,), (1,)), ((), ()))
GROUP = 16
PANEL = 16
STEP = 8


def split_rows(a, shape):
    lead = a.shape[:-2]
    a = jnp.swapaxes(a.reshape(lead + (4, 2, 128)), -3, -2)
    return a.reshape(shape)


def join_rows(a, shape):
    lead = shape[:-2]
    a = jnp.swapaxes(a.reshape(lead + (2, 4, 128)), -3, -2)
    return a.reshape(shape)


def typed(tissue):
    endo = tissue == 1
    mid = tissue == 2

    def pick(a, b, c):
        if a == b == c:
            return a
        if b == c:
            return jnp.where(endo, F32(a), F32(c))
        if a == c:
            return jnp.where(mid, F32(b), F32(c))
        if a == b:
            return jnp.where(tissue == 1, F32(a), jnp.where(mid, F32(a), F32(c)))
        return jnp.where(endo, F32(a), jnp.where(mid, F32(b), F32(c)))

    return pick


def each(fn, *columns):
    return tuple(fn(*entry) for entry in zip(*columns))


def collide(f, v, w, s, tissue, stim):
    pick = typed(tissue)
    live = tissue > 0
    u = ((f[0] + f[1]) + (f[2] + f[3])) + ((f[4] + f[5]) + f[6])
    hv = 0.5 + 0.5 * jnp.tanh(25.0 * (u - 0.3))
    hw = 0.5 + 0.5 * jnp.tanh(25.0 * (u - 0.13))
    hm = 0.5 + 0.5 * jnp.tanh(25.0 * (u - pick(0.2, 0.1, 0.006)))
    ho = 0.5 + 0.5 * jnp.tanh(25.0 * (u - pick(0.006, 0.005, 0.006)))
    nv, nw, no = 1.0 - hv, 1.0 - hw, 1.0 - ho
    tv1, tv2 = (75.0, 80.0, 60.0), (10.0, 1.4506, 1150.0)
    tvm = pick(*tv1) + hm * pick(*each(lambda a, b: b - a, tv1, tv2))
    tw1, tw2 = (6.0, 70.0, 60.0), (140.0, 8.0, 15.0)
    thw = jnp.tanh(pick(200.0, 200.0, 65.0) * (u - pick(0.016, 0.016, 0.03)))
    twm = pick(*each(lambda a, b: (a + b) / 2, tw1, tw2)) + thw * pick(
        *each(lambda a, b: (b - a) / 2, tw1, tw2)
    )
    ts1, ts2 = (40.0, 91.0, 30.0181), (1.2, 0.8, 0.9957)
    tht = jnp.tanh(pick(2.0, 2.1, 2.0458) * (u - pick(0.65, 0.6, 0.65)))
    tso = pick(*each(lambda a, b: (a + b) / 2, ts1, ts2)) + tht * pick(
        *each(lambda a, b: (b - a) / 2, ts1, ts2)
    )
    ts = 2.7342 + hw * pick(*each(lambda a: a - 2.7342, (2.0, 4.0, 16.0)))
    to1, to2 = (470.0, 410.0, 400.0), (6.0, 7.0, 6.0)
    to = pick(*to1) + ho * pick(*each(lambda a, b: b - a, to1, to2))
    winf = no * (1.0 - u * pick(*each(lambda a: 1 / a, (0.0273, 0.01, 0.07)))) + ho * pick(
        0.78, 0.5, 0.94
    )
    minus_fi = v * hv * (u - 0.3) * (pick(1.56, 1.61, 1.55) - u) * pick(
        *each(lambda a: 1 / a, (0.1, 0.078, 0.11))
    )
    outward = u * nw / to + hw / tso
    minus_si = hw * w * s * pick(*each(lambda a: 1 / a, (2.9013, 3.3849, 1.8875)))
    react = stim + minus_fi - outward + minus_si
    dv = nv * (1.0 - hm - v) / tvm - hv * v * (1 / 1.4506)
    dw = nw * (winf - w) / twm - hw * w * pick(*each(lambda a: 1 / a, (280.0, 280.0, 200.0)))
    ds = ((0.5 + 0.5 * jnp.tanh(2.0994 * (u - 0.9087))) - s) / ts
    gates = (
        jnp.where(live, v + DT * dv, v),
        jnp.where(live, w + DT * dw, w),
        jnp.where(live, s + DT * ds, s),
    )
    rate = pick(*each(lambda a: 1 / a, (0.95, 0.8, 1.1)))
    keep = pick(*each(lambda a: 1 - 1 / a, (0.95, 0.8, 1.1)))
    share = 0.125 * (u * rate + DT * react)
    g = [jnp.where(live, f[0] * keep + 2.0 * share, DEAD)]
    for i in range(1, 7):
        g.append(jnp.where(live, f[i] * keep + share, DEAD))
    return g, gates


def kernel(
    f_hbm, g_hbm, x_hbm, t_hbm, s_hbm, amp, rc,
    f_out, g_out, y_out, zt_ref, up_ref,
    fv, gv, xv, tv, sv, stim, cc, cxp, cxm, ysp, ysm, yrp, yrm, u1, u2,
    xs, red,
    load_sem, hs_sem, hr_sem, as_sem, ar_sem,
):
    planes = fv.shape[1]
    quads = planes // 4
    slabs, tiles = lax.axis_size("slab"), lax.axis_size("tile")
    slab, tile = lax.axis_index("slab"), lax.axis_index("tile")
    core, yy, zz = lax.rem(tile, 2), lax.rem(tile // 2, 4), tile // 8

    loads = [
        pltpu.make_async_copy(src, dst, load_sem.at[i])
        for i, (src, dst) in enumerate(
            ((x_hbm, xv), (f_hbm, fv), (t_hbm, tv), (s_hbm, sv), (g_hbm, gv))
        )
    ]
    for copy in loads:
        copy.start()

    right = (lax.rem(slab + 1, slabs), tile)
    left = (lax.rem(slab + slabs - 1, slabs), tile)
    up = (slab, lax.rem(tile + 1, tiles))
    down = (slab, lax.rem(tile + tiles - 1, tiles))
    rank = (slab * 4 + yy, zz * 2 + core)

    def partner(stage, k):
        other = lax.rem(rank[stage] + k, GROUP)
        if stage == 0:
            return (other // 4, zz * 8 + lax.rem(other, 4) * 2 + core)
        return (slab, other // 2 * 8 + yy * 2 + lax.rem(other, 2))

    barrier = pltpu.get_barrier_semaphore()
    for dev in (right, left, up, down):
        pl.semaphore_signal(barrier, inc=1, device_id=dev, device_id_type=MESH)
    for stage in range(2):

        def greet(k, carry, stage=stage):
            pl.semaphore_signal(barrier, inc=1, device_id=partner(stage, k), device_id_type=MESH)
            return carry

        lax.fori_loop(1, GROUP, greet, 0)

    row4 = lax.broadcasted_iota(jnp.int32, (8, 128), 0)
    lane = lax.broadcasted_iota(jnp.int32, (4, 8, 128), 2)
    row = lax.broadcasted_iota(jnp.int32, (4, 8, 128), 1)
    yrow = lax.rem(row, 4)
    yrow2 = lax.rem(row4, 4)

    def store_collided(step, q, g):
        p = pl.ds(q * 4, 4)
        cc[0, p] = g[0]
        cc[1, p] = g[3]
        cc[2, p] = g[4]
        cc[3, p] = g[5]
        cc[4, p] = g[6]
        cxp[step, pl.ds(q * 4 + 1, 4)] = g[1]
        cxm[step, p] = g[2]
        face_p = g[3][3]
        face_m = g[4][0]
        for k in range(3):
            face_p = jnp.where(yrow2 == k, pltpu.roll(g[3][k], 5 + k, 0), face_p)
        for k in range(1, 4):
            face_m = jnp.where(yrow2 == k, pltpu.roll(g[4][k], k, 0), face_m)
        ysp[step, q] = face_p
        ysm[step, q] = face_m

    def halos(step):
        pairs = (
            (cxp.at[step, pl.ds(planes, 1)], cxp.at[step, pl.ds(0, 1)], right),
            (cxm.at[step, pl.ds(0, 1)], cxm.at[step, pl.ds(planes, 1)], left),
            (ysp.at[step], yrp.at[step], up),
            (ysm.at[step], yrm.at[step], down),
        )
        return [
            pltpu.make_async_remote_copy(
                src_ref=src,
                dst_ref=dst,
                send_sem=hs_sem.at[step * 4 + i],
                recv_sem=hr_sem.at[step * 4 + i],
                device_id=dev,
                device_id_type=MESH,
            )
            for i, (src, dst, dev) in enumerate(pairs)
        ]

    def settle_halos(step):
        for copy in halos(step):
            copy.wait_recv()
        cxp[step, pl.ds(0, 1)] = jnp.where(slab == 0, DEAD, cxp[step, pl.ds(0, 1)])
        cxm[step, pl.ds(planes, 1)] = jnp.where(
            slab == slabs - 1, DEAD, cxm[step, pl.ds(planes, 1)]
        )
        yrp[step] = jnp.where(tile == 0, DEAD, yrp[step])
        yrm[step] = jnp.where(tile == tiles - 1, DEAD, yrm[step])

    def propagate(step, q, tissue):
        p = pl.ds(q * 4, 4)
        p1 = pl.ds(q * 4 + 1, 4)

        def bounce(moved, back):
            return jnp.where(moved > LIMIT, moved, back)

        gx1, gx2 = cxp[step, p1], cxm[step, p]
        gy1, gy2, gz1, gz2 = cc[1, p], cc[2, p], cc[3, p], cc[4, p]
        hp, hm = yrp[step, q], yrm[step, q]
        halo_p = jnp.stack([hp] + [pltpu.roll(hp, 8 - k, 0) for k in range(1, 4)])
        halo_m = jnp.stack([pltpu.roll(hm, 3 - k, 0) for k in range(3)] + [hm])
        my1 = jnp.where(yrow == 0, halo_p, pltpu.roll(gy1, 1, 1))
        my2 = jnp.where(yrow == 3, halo_m, pltpu.roll(gy2, 7, 1))
        rz1 = pltpu.roll(gz1, 1, 2)
        rz2 = pltpu.roll(gz2, 127, 2)
        mz1 = jnp.where(lane == 0, jnp.where(row >= 4, pltpu.roll(rz1, 4, 1), DEAD), rz1)
        mz2 = jnp.where(lane == 127, jnp.where(row < 4, pltpu.roll(rz2, 4, 1), DEAD), rz2)
        f = (
            cc[0, p],
            bounce(cxp[step, p], gx2),
            bounce(cxm[step, p1], gx1),
            bounce(my1, gy2),
            bounce(my2, gy1),
            bounce(mz1, gz2),
            bounce(mz2, gz1),
        )
        live = tissue > 0
        f = [jnp.where(live, part, 0.0) for part in f]
        u = ((f[0] + f[1]) + (f[2] + f[3])) + ((f[4] + f[5]) + f[6])
        return f, u

    def advance(q, f, current, gates_to):
        p = pl.ds(q * 4, 4)
        g, gates = collide(f, gv[0, p], gv[1, p], gv[2, p], tv[p], current)
        for i in range(3):
            gates_to[i, p] = gates[i]
        return g

    def reduce_copy(which, stage, slot, k):
        return pltpu.make_async_remote_copy(
            src_ref=slot,
            dst_ref=slot,
            send_sem=as_sem.at[which * 2 + stage],
            recv_sem=ar_sem.at[which * 2 + stage],
            device_id=partner(stage, k),
            device_id_type=MESH,
        )

    def reduce_send(which, stage, block):
        at = (which * 2 + stage) * GROUP + rank[stage]
        red[at] = block
        for k in range(1, GROUP):
            reduce_copy(which, stage, red.at[at], k).start()

    def reduce_all(which, stage):
        return reduce_copy(
            which, stage, red.at[pl.ds((which * 2 + stage) * GROUP, GROUP - 1)], 1
        )

    def reduce_sum(which, stage):
        reduce_all(which, stage).wait_recv()
        at = (which * 2 + stage) * GROUP
        parts = [red[at + i] for i in range(GROUP)]
        while len(parts) > 1:
            parts = [a + b for a, b in zip(parts[::2], parts[1::2])]
        return parts[0]

    def packed(m):
        return jnp.concatenate([m[8 * b : 8 * b + 8] for b in range(4)], axis=1)

    def unpacked(m):
        return jnp.concatenate([m[:, 32 * b : 32 * b + 32] for b in range(4)], axis=0)

    ri = lax.broadcasted_iota(jnp.int32, (32, 32), 0)
    ci = lax.broadcasted_iota(jnp.int32, (32, 32), 1)

    eye = jnp.where(ri == ci, 1.0, 0.0)

    def eliminate(a):
        m = jnp.concatenate([a, eye], axis=1)
        below = lax.broadcasted_iota(jnp.int32, (32, 64), 0)
        for p in range(0, 32, PANEL):
            cols = [jnp.broadcast_to(m[:, p + k : p + k + 1], (32, 64)) for k in range(PANEL)]
            rows = [m[p + k : p + k + 1, :] for k in range(PANEL)]
            taken_off = 0.0
            for k in range(PANEL):
                j = p + k
                low = jnp.where(below > j, cols[k] * (1.0 / cols[k][j : j + 1, :]), 0.0)
                for q in range(k + 1, PANEL):
                    cols[q] = cols[q] - low * cols[q][j : j + 1, :]
                    rows[q] = rows[q] - low[p + q : p + q + 1, :] * rows[k]
                taken_off = taken_off + low * rows[k]
            m = m - taken_off
        upper = m[:, :32]
        pivot = jnp.sum(jnp.where(ri == ci, upper, 0.0), axis=1, keepdims=True)
        return jnp.where(ri <= ci, upper, 0.0), m[:, 32:], pivot

    wide_row = lax.broadcasted_iota(jnp.int32, (256, 256), 0)
    wide_col = lax.broadcasted_iota(jnp.int32, (256, 256), 1)
    same = lax.rem(wide_row, 8) == lax.rem(wide_col, 8)

    def folded(p):
        m = jnp.sum(jnp.where(same, p, 0.0).reshape(32, 8, 256), axis=1)
        place = lax.broadcasted_iota(jnp.int32, (256, 32), 0) // 8
        pick = jnp.where(place == lax.broadcasted_iota(jnp.int32, (256, 32), 1), 1.0, 0.0)
        return jnp.dot(m, pick, precision=lax.Precision.HIGHEST, preferred_element_type=F32)

    loads[0].wait()

    def pair(x):
        return jnp.concatenate([xv[:, 2 * x].reshape(256, 128), xv[:, 2 * x + 1].reshape(256, 128)], axis=1)

    def old_gram(i, acc):
        parts = [pair(STEP * i + k).astype(BF16) for k in range(STEP)]
        for k in range(STEP):
            xs[STEP * i + k, :256] = parts[k]
        hi = jnp.concatenate(parts, axis=1)
        return acc + lax.dot_general(hi, hi, NT, preferred_element_type=F32)

    acc = lax.fori_loop(0, planes // 2 // STEP, old_gram, jnp.zeros((256, 256), F32))
    block = packed(folded(acc))
    pl.semaphore_wait(barrier, 4 + 2 * (GROUP - 1))
    reduce_send(0, 0, block)

    for copy in loads[1:]:
        copy.wait()

    def first(q, carry):
        p = pl.ds(q * 4, 4)
        site = sv[p]
        current = jnp.zeros((4, 8, 128), F32)
        for k in range(8):
            current = jnp.where(site == k + 1, amp[k], current)
        stim[p] = current
        store_collided(0, q, advance(q, [fv[i, p] for i in range(7)], current, gv))
        return carry

    lax.fori_loop(0, quads, first, 0)
    for copy in halos(0):
        copy.start()

    def finer(i, carry):
        rest = pair(i) - xs[i, :256].astype(F32)
        mid = rest.astype(BF16)
        xs[i, 256:512] = mid
        xs[i, 512:] = (rest - mid.astype(F32)).astype(BF16)
        return carry

    lax.fori_loop(0, planes // 2, finer, 0)

    reduce_send(0, 1, reduce_sum(0, 0))

    settle_halos(0)

    def second(q, carry):
        p = pl.ds(q * 4, 4)
        f, u = propagate(0, q, tv[p])
        u1[p] = u
        store_collided(1, q, advance(q, f, stim[p], g_out))
        return carry

    lax.fori_loop(0, quads, second, 0)
    for copy in halos(1):
        copy.start()

    gram = unpacked(reduce_sum(0, 1))
    taken = (ri == rc[0]) | (ri == rc[1]) | (ci == rc[0]) | (ci == rc[1])
    gram = jnp.where(taken, eye, gram * (1.0 + eye * 2.0**-16))
    _, inv0, pivot = eliminate(gram)
    t0 = (inv0 * (1.0 / jnp.sqrt(pivot))).astype(BF16)
    spread = spread_rows(t0, True, False)
    spread = jnp.concatenate([spread, spread, spread], axis=1)

    settle_halos(1)

    def fourth(q, carry):
        p = pl.ds(q * 4, 4)
        f, u = propagate(1, q, tv[p])
        u2[p] = u
        for i in range(7):
            f_out[i, p] = f[i]
        return carry

    lax.fori_loop(0, quads, fourth, 0)

    column = lax.broadcasted_iota(jnp.int32, (32, 256), 0)
    is1, is2 = column == rc[0], column == rc[1]

    def new_gram(i, acc):
        his, los = [], []
        for k in range(STEP):
            at = STEP * i + k
            y = jnp.dot(spread, xs[at], preferred_element_type=F32)
            new1 = jnp.concatenate([u1[2 * at], u1[2 * at + 1]], axis=1)
            new2 = jnp.concatenate([u2[2 * at], u2[2 * at + 1]], axis=1)
            for r in range(8):
                part = y[32 * r : 32 * r + 32]
                part = jnp.where(is2, new2[r : r + 1], part)
                part = jnp.where(is1, new1[r : r + 1], part)
                hi = part.astype(BF16)
                lo = (part - hi.astype(F32)).astype(BF16)
                y_out[at, 0, 32 * r : 32 * r + 32] = hi
                y_out[at, 1, 32 * r : 32 * r + 32] = lo
                his.append(hi)
                los.append(lo)
        both = jnp.concatenate(
            [jnp.concatenate(his, axis=1), jnp.concatenate(los, axis=1)], axis=0
        )
        return acc + lax.dot_general(both, both, NT, preferred_element_type=F32)

    acc = lax.fori_loop(0, planes // 2 // STEP, new_gram, jnp.zeros((64, 64), F32))
    gram = acc[:32, :32] + ((acc[:32, 32:] + acc[32:, :32]) + acc[32:, 32:])
    reduce_send(1, 0, packed(gram))
    _, inv0, pivot = eliminate(t0.astype(F32))
    back = inv0 * (1.0 / pivot)
    reduce_send(1, 1, reduce_sum(1, 0))
    r2, inv2, pivot = eliminate(unpacked(reduce_sum(1, 1)))
    scale = 1.0 / jnp.sqrt(pivot)
    norm = math.sqrt(planes * 1024 * slabs * tiles)
    zt_ref[...] = inv2 * (scale * norm)
    up_ref[...] = lax.dot_general(
        r2 * scale, back, NT, precision=lax.Precision.HIGHEST, preferred_element_type=F32
    ) * (1.0 / norm)

    for step in range(2):
        for copy in halos(step):
            copy.wait_send()
    for which in range(2):
        for stage in range(2):
            reduce_all(which, stage).wait_send()


def places(shape, dim, row_first):
    at = lax.broadcasted_iota(jnp.int32, shape, dim)
    return (at // 32, lax.rem(at, 32)) if row_first else (lax.rem(at, 8), at // 8)


def spread_rows(t, out_row_first, in_row_first):
    index = lax.broadcasted_iota(jnp.int32, (256, 32), 1)

    def pick(row_first):
        return jnp.where(places((256, 32), 0, row_first)[1] == index, 1.0, 0.0).astype(BF16)

    half = jnp.dot(pick(out_row_first), t, preferred_element_type=F32).astype(BF16)
    full = lax.dot_general(half, pick(in_row_first), NT, preferred_element_type=F32)
    same = places((256, 256), 0, out_row_first)[0] == places((256, 256), 1, in_row_first)[0]
    return jnp.where(same, full, 0.0).astype(BF16)


def basis_kernel(
    y_ref, f_ref, g_ref, z_ref, r_ref, q_hbm, f_hbm, g_hbm, r_hbm, qv, q_sem, p_sem
):
    parts = q_sem.shape[0]
    pairs = y_ref.shape[0] // parts
    passed = [
        pltpu.make_async_copy(src, dst, p_sem.at[i])
        for i, (src, dst) in enumerate(((f_ref, f_hbm), (g_ref, g_hbm), (r_ref, r_hbm)))
    ]
    for copy in passed:
        copy.start()
    z = z_ref[...]
    hi = z.astype(BF16)
    spread = spread_rows(hi, False, True)
    rest = spread_rows((z - hi.astype(F32)).astype(BF16), False, True)
    wide = jnp.concatenate([spread, spread, rest], axis=1)
    stores = []
    for i in range(parts):
        for k in range(pairs):
            at = i * pairs + k
            tall = jnp.concatenate([y_ref[at, 0], y_ref[at, 1], y_ref[at, 0]], axis=0)
            q = jnp.dot(wide, tall, preferred_element_type=F32)
            for j in range(2):
                qv[:, 2 * at + j] = q[:, 128 * j : 128 * j + 128].reshape(32, 8, 128)
        planes = pl.ds(2 * i * pairs, 2 * pairs)
        stores.append(
            pltpu.make_async_copy(qv.at[:, planes], q_hbm.at[:, planes], q_sem.at[i])
        )
        stores[-1].start()
    for copy in passed + stores:
        copy.wait()


def local(distributions, gate_states, history, tissue, stim_site, stim_amp, record_column):
    planes = distributions.shape[1]
    hbm = pl.BlockSpec(memory_space=pltpu.HBM)
    any_space = pl.BlockSpec(memory_space=pl.ANY)
    smem = pl.BlockSpec(memory_space=pltpu.SMEM)
    vmem = pl.BlockSpec(memory_space=pltpu.VMEM)
    grid_f = (7, planes, 8, 128)
    shapes = [
        pltpu.VMEM(grid_f, F32),
        pltpu.VMEM((3, planes, 8, 128), F32),
        pltpu.VMEM((planes // 2, 2, 256, 256), BF16),
        pltpu.VMEM((32, 32), F32),
        pltpu.VMEM((32, 32), F32),
    ]
    plane = (planes, 8, 128)
    scratch = [
        pltpu.VMEM(grid_f, F32),
        pltpu.VMEM((3,) + plane, F32),
        pltpu.VMEM((32,) + plane, F32),
        pltpu.VMEM(plane, jnp.int32),
        pltpu.VMEM(plane, jnp.int32),
        pltpu.VMEM(plane, F32),
        pltpu.VMEM((5,) + plane, F32),
        pltpu.VMEM((2, planes + 1, 8, 128), F32),
        pltpu.VMEM((2, planes + 1, 8, 128), F32),
        pltpu.VMEM((2, planes // 4, 8, 128), F32),
        pltpu.VMEM((2, planes // 4, 8, 128), F32),
        pltpu.VMEM((2, planes // 4, 8, 128), F32),
        pltpu.VMEM((2, planes // 4, 8, 128), F32),
        pltpu.VMEM(plane, F32),
        pltpu.VMEM(plane, F32),
        pltpu.VMEM((planes // 2, 768, 256), BF16),
        pltpu.VMEM((4 * GROUP, 8, 128), F32),
        pltpu.SemaphoreType.DMA((5,)),
        pltpu.SemaphoreType.DMA((8,)),
        pltpu.SemaphoreType.DMA((8,)),
        pltpu.SemaphoreType.DMA((4,)),
        pltpu.SemaphoreType.DMA((4,)),
    ]
    f, g, y, zt, up = pl.pallas_call(
        kernel,
        out_shape=shapes,
        in_specs=[hbm] * 5 + [smem] * 2,
        out_specs=[vmem] * 5,
        scratch_shapes=scratch,
        compiler_params=pltpu.CompilerParams(
            collective_id=0, has_side_effects=True, vmem_limit_bytes=54 << 20
        ),
    )(
        split_rows(distributions, grid_f),
        split_rows(gate_states, (3,) + plane),
        split_rows(history, (32,) + plane),
        split_rows(tissue, plane),
        split_rows(stim_site, plane),
        stim_amp,
        record_column,
    )
    parts = 8
    q, f, g, up = pl.pallas_call(
        basis_kernel,
        out_shape=[
            jax.ShapeDtypeStruct((32,) + plane, F32),
            jax.ShapeDtypeStruct(grid_f, F32),
            jax.ShapeDtypeStruct((3,) + plane, F32),
            jax.ShapeDtypeStruct((32, 32), F32),
        ],
        in_specs=[vmem] * 5,
        out_specs=[any_space] * 4,
        scratch_shapes=[
            pltpu.VMEM((32,) + plane, F32),
            pltpu.SemaphoreType.DMA((parts,)),
            pltpu.SemaphoreType.DMA((3,)),
        ],
        compiler_params=pltpu.CompilerParams(vmem_limit_bytes=48 << 20),
    )(y, f, g, zt, up)
    return (
        join_rows(f, distributions.shape),
        join_rows(g, gate_states.shape),
        join_rows(q, history.shape),
        up,
    )


def solution(mesh):
    field = P(None, "slab", "tile", None)
    label = P("slab", "tile", None)
    return jax.shard_map(
        local,
        mesh=mesh,
        in_specs=(field, field, field, label, label, P(), P()),
        out_specs=(field, field, field, P()),
        check_vma=False,
    )
```

```python
import functools
import math

import jax
import jax.numpy as jnp
from jax import lax
from jax.experimental import pallas as pl
from jax.experimental.pallas import tpu as pltpu
from jax.sharding import PartitionSpec as P

MESH = pl.DeviceIdType.MESH
DT = 0.1
DEAD = -1e30
LIMIT = -1e29
F32 = jnp.float32
BF16 = jnp.bfloat16
NT = (((1,), (1,)), ((), ()))
GROUP = 16
PANEL = 16
STEP = 8


def split_rows(a, shape):
    lead = a.shape[:-2]
    a = jnp.swapaxes(a.reshape(lead + (4, 2, 128)), -3, -2)
    return a.reshape(shape)


def join_rows(a, shape):
    lead = shape[:-2]
    a = jnp.swapaxes(a.reshape(lead + (2, 4, 128)), -3, -2)
    return a.reshape(shape)


def typed(tissue):
    endo = tissue == 1
    mid = tissue == 2

    def pick(a, b, c):
        if a == b == c:
            return a
        if b == c:
            return jnp.where(endo, F32(a), F32(c))
        if a == c:
            return jnp.where(mid, F32(b), F32(c))
        if a == b:
            return jnp.where(tissue == 1, F32(a), jnp.where(mid, F32(a), F32(c)))
        return jnp.where(endo, F32(a), jnp.where(mid, F32(b), F32(c)))

    return pick


def each(fn, *columns):
    return tuple(fn(*entry) for entry in zip(*columns))


def collide(f, v, w, s, tissue, stim):
    pick = typed(tissue)
    live = tissue > 0
    u = ((f[0] + f[1]) + (f[2] + f[3])) + ((f[4] + f[5]) + f[6])
    hv = 0.5 + 0.5 * jnp.tanh(25.0 * (u - 0.3))
    hw = 0.5 + 0.5 * jnp.tanh(25.0 * (u - 0.13))
    hm = 0.5 + 0.5 * jnp.tanh(25.0 * (u - pick(0.2, 0.1, 0.006)))
    ho = 0.5 + 0.5 * jnp.tanh(25.0 * (u - pick(0.006, 0.005, 0.006)))
    nv, nw, no = 1.0 - hv, 1.0 - hw, 1.0 - ho
    tv1, tv2 = (75.0, 80.0, 60.0), (10.0, 1.4506, 1150.0)
    tvm = pick(*tv1) + hm * pick(*each(lambda a, b: b - a, tv1, tv2))
    tw1, tw2 = (6.0, 70.0, 60.0), (140.0, 8.0, 15.0)
    thw = jnp.tanh(pick(200.0, 200.0, 65.0) * (u - pick(0.016, 0.016, 0.03)))
    twm = pick(*each(lambda a, b: (a + b) / 2, tw1, tw2)) + thw * pick(
        *each(lambda a, b: (b - a) / 2, tw1, tw2)
    )
    ts1, ts2 = (40.0, 91.0, 30.0181), (1.2, 0.8, 0.9957)
    tht = jnp.tanh(pick(2.0, 2.1, 2.0458) * (u - pick(0.65, 0.6, 0.65)))
    tso = pick(*each(lambda a, b: (a + b) / 2, ts1, ts2)) + tht * pick(
        *each(lambda a, b: (b - a) / 2, ts1, ts2)
    )
    ts = 2.7342 + hw * pick(*each(lambda a: a - 2.7342, (2.0, 4.0, 16.0)))
    to1, to2 = (470.0, 410.0, 400.0), (6.0, 7.0, 6.0)
    to = pick(*to1) + ho * pick(*each(lambda a, b: b - a, to1, to2))
    winf = no * (1.0 - u * pick(*each(lambda a: 1 / a, (0.0273, 0.01, 0.07)))) + ho * pick(
        0.78, 0.5, 0.94
    )
    minus_fi = v * hv * (u - 0.3) * (pick(1.56, 1.61, 1.55) - u) * pick(
        *each(lambda a: 1 / a, (0.1, 0.078, 0.11))
    )
    outward = u * nw / to + hw / tso
    minus_si = hw * w * s * pick(*each(lambda a: 1 / a, (2.9013, 3.3849, 1.8875)))
    react = stim + minus_fi - outward + minus_si
    dv = nv * (1.0 - hm - v) / tvm - hv * v * (1 / 1.4506)
    dw = nw * (winf - w) / twm - hw * w * pick(*each(lambda a: 1 / a, (280.0, 280.0, 200.0)))
    ds = ((0.5 + 0.5 * jnp.tanh(2.0994 * (u - 0.9087))) - s) / ts
    gates = (
        jnp.where(live, v + DT * dv, v),
        jnp.where(live, w + DT * dw, w),
        jnp.where(live, s + DT * ds, s),
    )
    rate = pick(*each(lambda a: 1 / a, (0.95, 0.8, 1.1)))
    keep = pick(*each(lambda a: 1 - 1 / a, (0.95, 0.8, 1.1)))
    share = 0.125 * (u * rate + DT * react)
    g = [jnp.where(live, f[0] * keep + 2.0 * share, DEAD)]
    for i in range(1, 7):
        g.append(jnp.where(live, f[i] * keep + share, DEAD))
    return g, gates


def kernel(
    f_hbm, g_hbm, x_hbm, t_hbm, s_hbm, amp_hbm, rc_hbm,
    f_out, g_out, y_out, zt_ref, r2_ref, back_ref,
    fv, gv, xv, tv, sv, stim, cc, cxp, cxm, ysp, ysm, yrp, yrm, u1, u2,
    xs, red, amp, rc,
    load_sem, hs_sem, hr_sem, as_sem, ar_sem,
):
    planes = fv.shape[1]
    quads = planes // 4
    slabs, tiles = lax.axis_size("slab"), lax.axis_size("tile")
    slab, tile = lax.axis_index("slab"), lax.axis_index("tile")
    core, yy, zz = lax.rem(tile, 2), lax.rem(tile // 2, 4), tile // 8

    halves = [pl.ds(i * (planes // 2), planes // 2) for i in range(2)]
    loads = [
        pltpu.make_async_copy(src, dst, load_sem.at[i])
        for i, (src, dst) in enumerate(
            [(x_hbm.at[:, half], xv.at[:, half]) for half in halves]
            + [(f_hbm, fv), (t_hbm, tv), (s_hbm, sv), (g_hbm, gv), (amp_hbm, amp), (rc_hbm, rc)]
        )
    ]
    for copy in loads:
        copy.start()

    right = (lax.rem(slab + 1, slabs), tile)
    left = (lax.rem(slab + slabs - 1, slabs), tile)
    up = (slab, lax.rem(tile + 1, tiles))
    down = (slab, lax.rem(tile + tiles - 1, tiles))
    rank = (slab * 4 + yy, zz * 2 + core)

    def partner(stage, k):
        other = lax.rem(rank[stage] + k, GROUP)
        if stage == 0:
            return (other // 4, zz * 8 + lax.rem(other, 4) * 2 + core)
        return (slab, other // 2 * 8 + yy * 2 + lax.rem(other, 2))

    barrier = pltpu.get_barrier_semaphore()
    for dev in (right, left, up, down):
        pl.semaphore_signal(barrier, inc=1, device_id=dev, device_id_type=MESH)
    for stage in range(2):

        def greet(k, carry, stage=stage):
            pl.semaphore_signal(barrier, inc=1, device_id=partner(stage, k), device_id_type=MESH)
            return carry

        lax.fori_loop(1, GROUP, greet, 0)

    row4 = lax.broadcasted_iota(jnp.int32, (8, 128), 0)
    lane = lax.broadcasted_iota(jnp.int32, (4, 8, 128), 2)
    row = lax.broadcasted_iota(jnp.int32, (4, 8, 128), 1)
    yrow = lax.rem(row, 4)
    yrow2 = lax.rem(row4, 4)

    def store_collided(step, q, g):
        p = pl.ds(q * 4, 4)
        cc[0, p] = g[0]
        cc[1, p] = g[3]
        cc[2, p] = g[4]
        cc[3, p] = g[5]
        cc[4, p] = g[6]
        cxp[step, pl.ds(q * 4 + 1, 4)] = g[1]
        cxm[step, p] = g[2]
        face_p = g[3][3]
        face_m = g[4][0]
        for k in range(3):
            face_p = jnp.where(yrow2 == k, pltpu.roll(g[3][k], 5 + k, 0), face_p)
        for k in range(1, 4):
            face_m = jnp.where(yrow2 == k, pltpu.roll(g[4][k], k, 0), face_m)
        ysp[step, q] = face_p
        ysm[step, q] = face_m

    def halos(step):
        pairs = (
            (cxp.at[step, pl.ds(planes, 1)], cxp.at[step, pl.ds(0, 1)], right),
            (cxm.at[step, pl.ds(0, 1)], cxm.at[step, pl.ds(planes, 1)], left),
            (ysp.at[step], yrp.at[step], up),
            (ysm.at[step], yrm.at[step], down),
        )
        return [
            pltpu.make_async_remote_copy(
                src_ref=src,
                dst_ref=dst,
                send_sem=hs_sem.at[step * 4 + i],
                recv_sem=hr_sem.at[step * 4 + i],
                device_id=dev,
                device_id_type=MESH,
            )
            for i, (src, dst, dev) in enumerate(pairs)
        ]

    def settle_halos(step):
        for copy in halos(step):
            copy.wait_recv()
        cxp[step, pl.ds(0, 1)] = jnp.where(slab == 0, DEAD, cxp[step, pl.ds(0, 1)])
        cxm[step, pl.ds(planes, 1)] = jnp.where(
            slab == slabs - 1, DEAD, cxm[step, pl.ds(planes, 1)]
        )
        yrp[step] = jnp.where(tile == 0, DEAD, yrp[step])
        yrm[step] = jnp.where(tile == tiles - 1, DEAD, yrm[step])

    def propagate(step, q, tissue):
        p = pl.ds(q * 4, 4)
        p1 = pl.ds(q * 4 + 1, 4)

        def bounce(moved, back):
            return jnp.where(moved > LIMIT, moved, back)

        gx1, gx2 = cxp[step, p1], cxm[step, p]
        gy1, gy2, gz1, gz2 = cc[1, p], cc[2, p], cc[3, p], cc[4, p]
        hp, hm = yrp[step, q], yrm[step, q]
        halo_p = jnp.stack([hp] + [pltpu.roll(hp, 8 - k, 0) for k in range(1, 4)])
        halo_m = jnp.stack([pltpu.roll(hm, 3 - k, 0) for k in range(3)] + [hm])
        my1 = jnp.where(yrow == 0, halo_p, pltpu.roll(gy1, 1, 1))
        my2 = jnp.where(yrow == 3, halo_m, pltpu.roll(gy2, 7, 1))
        rz1 = pltpu.roll(gz1, 1, 2)
        rz2 = pltpu.roll(gz2, 127, 2)
        mz1 = jnp.where(lane == 0, jnp.where(row >= 4, pltpu.roll(rz1, 4, 1), DEAD), rz1)
        mz2 = jnp.where(lane == 127, jnp.where(row < 4, pltpu.roll(rz2, 4, 1), DEAD), rz2)
        f = (
            cc[0, p],
            bounce(cxp[step, p], gx2),
            bounce(cxm[step, p1], gx1),
            bounce(my1, gy2),
            bounce(my2, gy1),
            bounce(mz1, gz2),
            bounce(mz2, gz1),
        )
        live = tissue > 0
        f = [jnp.where(live, part, 0.0) for part in f]
        u = ((f[0] + f[1]) + (f[2] + f[3])) + ((f[4] + f[5]) + f[6])
        return f, u

    def advance(q, f, current, gates_to):
        p = pl.ds(q * 4, 4)
        g, gates = collide(f, gv[0, p], gv[1, p], gv[2, p], tv[p], current)
        for i in range(3):
            gates_to[i, p] = gates[i]
        return g

    def reduce_copy(which, stage, slot, k):
        return pltpu.make_async_remote_copy(
            src_ref=slot,
            dst_ref=slot,
            send_sem=as_sem.at[which * 2 + stage],
            recv_sem=ar_sem.at[which * 2 + stage],
            device_id=partner(stage, k),
            device_id_type=MESH,
        )

    def reduce_send(which, stage, block):
        at = (which * 2 + stage) * GROUP + rank[stage]
        red[at] = block
        for k in range(1, GROUP):
            reduce_copy(which, stage, red.at[at], k).start()

    def reduce_all(which, stage):
        return reduce_copy(
            which, stage, red.at[pl.ds((which * 2 + stage) * GROUP, GROUP - 1)], 1
        )

    def reduce_sum(which, stage):
        reduce_all(which, stage).wait_recv()
        at = (which * 2 + stage) * GROUP
        parts = [red[at + i] for i in range(GROUP)]
        while len(parts) > 1:
            parts = [a + b for a, b in zip(parts[::2], parts[1::2])]
        return parts[0]

    def packed(m):
        return jnp.concatenate([m[8 * b : 8 * b + 8] for b in range(4)], axis=1)

    def unpacked(m):
        return jnp.concatenate([m[:, 32 * b : 32 * b + 32] for b in range(4)], axis=0)

    ri = lax.broadcasted_iota(jnp.int32, (32, 32), 0)
    ci = lax.broadcasted_iota(jnp.int32, (32, 32), 1)

    eye = jnp.where(ri == ci, 1.0, 0.0)

    def eliminate(a):
        m = jnp.concatenate([a, eye], axis=1)
        below = lax.broadcasted_iota(jnp.int32, (32, 64), 0)
        for p in range(0, 32, PANEL):
            cols = [jnp.broadcast_to(m[:, p + k : p + k + 1], (32, 64)) for k in range(PANEL)]
            rows = [m[p + k : p + k + 1, :] for k in range(PANEL)]
            taken_off = 0.0
            for k in range(PANEL):
                j = p + k
                low = jnp.where(below > j, cols[k] * (1.0 / cols[k][j : j + 1, :]), 0.0)
                for q in range(k + 1, PANEL):
                    cols[q] = cols[q] - low * cols[q][j : j + 1, :]
                    rows[q] = rows[q] - low[p + q : p + q + 1, :] * rows[k]
                taken_off = taken_off + low * rows[k]
            m = m - taken_off
        upper = m[:, :32]
        pivot = jnp.sum(jnp.where(ri == ci, upper, 0.0), axis=1, keepdims=True)
        return jnp.where(ri <= ci, upper, 0.0), m[:, 32:], pivot

    wide_row = lax.broadcasted_iota(jnp.int32, (256, 256), 0)
    wide_col = lax.broadcasted_iota(jnp.int32, (256, 256), 1)
    same = lax.rem(wide_row, 8) == lax.rem(wide_col, 8)

    def folded(p):
        m = jnp.sum(jnp.where(same, p, 0.0).reshape(32, 8, 256), axis=1)
        place = lax.broadcasted_iota(jnp.int32, (256, 32), 0) // 8
        pick = jnp.where(place == lax.broadcasted_iota(jnp.int32, (256, 32), 1), 1.0, 0.0)
        return jnp.dot(m, pick, precision=lax.Precision.HIGHEST, preferred_element_type=F32)


    def pair(x):
        return jnp.concatenate([xv[:, 2 * x].reshape(256, 128), xv[:, 2 * x + 1].reshape(256, 128)], axis=1)

    def old_gram(i, acc):
        parts = [pair(STEP * i + k).astype(BF16) for k in range(STEP)]
        for k in range(STEP):
            xs[STEP * i + k, :256] = parts[k]
        hi = jnp.concatenate(parts, axis=1)
        return acc + lax.dot_general(hi, hi, NT, preferred_element_type=F32)

    share = planes // 4 // STEP
    acc = jnp.zeros((256, 256), F32)
    for half in range(2):
        loads[half].wait()
        acc = lax.fori_loop(half * share, (half + 1) * share, old_gram, acc)
    block = packed(folded(acc))
    pl.semaphore_wait(barrier, 4 + 2 * (GROUP - 1))
    reduce_send(0, 0, block)

    for copy in loads[2:]:
        copy.wait()

    def first(q, carry):
        p = pl.ds(q * 4, 4)
        site = sv[p]
        current = jnp.zeros((4, 8, 128), F32)
        for k in range(8):
            current = jnp.where(site == k + 1, amp[k], current)
        stim[p] = current
        store_collided(0, q, advance(q, [fv[i, p] for i in range(7)], current, gv))
        return carry

    lax.fori_loop(0, quads, first, 0)
    for copy in halos(0):
        copy.start()

    def finer(i, carry):
        rest = pair(i) - xs[i, :256].astype(F32)
        mid = rest.astype(BF16)
        xs[i, 256:512] = mid
        xs[i, 512:] = (rest - mid.astype(F32)).astype(BF16)
        return carry

    lax.fori_loop(0, planes // 2, finer, 0)

    reduce_send(0, 1, reduce_sum(0, 0))

    settle_halos(0)

    def second(q, carry):
        p = pl.ds(q * 4, 4)
        f, u = propagate(0, q, tv[p])
        u1[p] = u
        store_collided(1, q, advance(q, f, stim[p], g_out))
        return carry

    lax.fori_loop(0, quads, second, 0)
    for copy in halos(1):
        copy.start()

    settle_halos(1)

    def fourth(q, carry):
        p = pl.ds(q * 4, 4)
        f, u = propagate(1, q, tv[p])
        u2[p] = u
        for i in range(7):
            f_out[i, p] = f[i]
        return carry

    lax.fori_loop(0, quads, fourth, 0)

    gram = unpacked(reduce_sum(0, 1))
    taken = (ri == rc[0]) | (ri == rc[1]) | (ci == rc[0]) | (ci == rc[1])
    gram = jnp.where(taken, eye, gram * (1.0 + eye * 2.0**-16))
    _, inv0, pivot = eliminate(gram)
    t0 = (inv0 * (1.0 / jnp.sqrt(pivot))).astype(BF16)
    spread = spread_rows(t0, True, False)
    spread = jnp.concatenate([spread, spread, spread], axis=1)

    column = lax.broadcasted_iota(jnp.int32, (32, 256), 0)
    is1, is2 = column == rc[0], column == rc[1]

    def new_gram(i, acc):
        his, los = [], []
        for k in range(STEP):
            at = STEP * i + k
            y = jnp.dot(spread, xs[at], preferred_element_type=F32)
            new1 = jnp.concatenate([u1[2 * at], u1[2 * at + 1]], axis=1)
            new2 = jnp.concatenate([u2[2 * at], u2[2 * at + 1]], axis=1)
            for r in range(8):
                part = y[32 * r : 32 * r + 32]
                part = jnp.where(is2, new2[r : r + 1], part)
                part = jnp.where(is1, new1[r : r + 1], part)
                hi = part.astype(BF16)
                lo = (part - hi.astype(F32)).astype(BF16)
                y_out[at, 0, 32 * r : 32 * r + 32] = hi
                y_out[at, 1, 32 * r : 32 * r + 32] = lo
                his.append(hi)
                los.append(lo)
        both = jnp.concatenate(
            [jnp.concatenate(his, axis=1), jnp.concatenate(los, axis=1)], axis=0
        )
        return acc + lax.dot_general(both, both, NT, preferred_element_type=F32)

    acc = lax.fori_loop(0, planes // 2 // STEP, new_gram, jnp.zeros((64, 64), F32))
    gram = acc[:32, :32] + ((acc[:32, 32:] + acc[32:, :32]) + acc[32:, 32:])
    reduce_send(1, 0, packed(gram))
    _, inv0, pivot = eliminate(t0.astype(F32))
    back_ref[...] = inv0 * (1.0 / pivot)
    reduce_send(1, 1, reduce_sum(1, 0))
    r2, inv2, pivot = eliminate(unpacked(reduce_sum(1, 1)))
    scale = 1.0 / jnp.sqrt(pivot)
    norm = math.sqrt(planes * 1024 * slabs * tiles)
    zt_ref[...] = inv2 * (scale * norm)
    r2_ref[...] = r2 * (scale * (1.0 / norm))

    for step in range(2):
        for copy in halos(step):
            copy.wait_send()
    for which in range(2):
        for stage in range(2):
            reduce_all(which, stage).wait_send()


def places(shape, dim, row_first):
    at = lax.broadcasted_iota(jnp.int32, shape, dim)
    return (at // 32, lax.rem(at, 32)) if row_first else (lax.rem(at, 8), at // 8)


def spread_rows(t, out_row_first, in_row_first):
    index = lax.broadcasted_iota(jnp.int32, (256, 32), 1)

    def pick(row_first):
        return jnp.where(places((256, 32), 0, row_first)[1] == index, 1.0, 0.0).astype(BF16)

    half = jnp.dot(pick(out_row_first), t, preferred_element_type=F32).astype(BF16)
    full = lax.dot_general(half, pick(in_row_first), NT, preferred_element_type=F32)
    same = places((256, 256), 0, out_row_first)[0] == places((256, 256), 1, in_row_first)[0]
    return jnp.where(same, full, 0.0).astype(BF16)


def basis_kernel(
    y_ref, f_ref, g_ref, z_ref, r2_ref, back_ref,
    q_hbm, f_hbm, g_hbm, up_hbm, qv, up, q_sem, p_sem,
):
    parts = q_sem.shape[0]
    pairs = y_ref.shape[0] // parts
    passed = [
        pltpu.make_async_copy(src, dst, p_sem.at[i])
        for i, (src, dst) in enumerate(((f_ref, f_hbm), (g_ref, g_hbm), (up, up_hbm)))
    ]
    for copy in passed[:2]:
        copy.start()
    z = z_ref[...]
    hi = z.astype(BF16)
    spread = spread_rows(hi, False, True)
    rest = spread_rows((z - hi.astype(F32)).astype(BF16), False, True)
    wide = jnp.concatenate([spread, spread, rest], axis=1)
    stores = []
    for i in range(parts):
        for k in range(pairs):
            at = i * pairs + k
            tall = jnp.concatenate([y_ref[at, 0], y_ref[at, 1], y_ref[at, 0]], axis=0)
            q = jnp.dot(wide, tall, preferred_element_type=F32)
            for j in range(2):
                qv[:, 2 * at + j] = q[:, 128 * j : 128 * j + 128].reshape(32, 8, 128)
        planes = pl.ds(2 * i * pairs, 2 * pairs)
        stores.append(
            pltpu.make_async_copy(qv.at[:, planes], q_hbm.at[:, planes], q_sem.at[i])
        )
        stores[-1].start()
        if i == parts // 2:
            up[...] = lax.dot_general(
                r2_ref[...],
                back_ref[...],
                NT,
                precision=lax.Precision.HIGHEST,
                preferred_element_type=F32,
            )
            passed[2].start()
    for copy in passed + stores:
        copy.wait()


def local(distributions, gate_states, history, tissue, stim_site, stim_amp, record_column):
    planes = distributions.shape[1]
    hbm = pl.BlockSpec(memory_space=pltpu.HBM)
    any_space = pl.BlockSpec(memory_space=pl.ANY)
    vmem = pl.BlockSpec(memory_space=pltpu.VMEM)
    grid_f = (7, planes, 8, 128)
    shapes = [
        pltpu.VMEM(grid_f, F32),
        pltpu.VMEM((3, planes, 8, 128), F32),
        pltpu.VMEM((planes // 2, 2, 256, 256), BF16),
        pltpu.VMEM((32, 32), F32),
        pltpu.VMEM((32, 32), F32),
        pltpu.VMEM((32, 32), F32),
    ]
    plane = (planes, 8, 128)
    scratch = [
        pltpu.VMEM(grid_f, F32),
        pltpu.VMEM((3,) + plane, F32),
        pltpu.VMEM((32,) + plane, F32),
        pltpu.VMEM(plane, jnp.int32),
        pltpu.VMEM(plane, jnp.int32),
        pltpu.VMEM(plane, F32),
        pltpu.VMEM((5,) + plane, F32),
        pltpu.VMEM((2, planes + 1, 8, 128), F32),
        pltpu.VMEM((2, planes + 1, 8, 128), F32),
        pltpu.VMEM((2, planes // 4, 8, 128), F32),
        pltpu.VMEM((2, planes // 4, 8, 128), F32),
        pltpu.VMEM((2, planes // 4, 8, 128), F32),
        pltpu.VMEM((2, planes // 4, 8, 128), F32),
        pltpu.VMEM(plane, F32),
        pltpu.VMEM(plane, F32),
        pltpu.VMEM((planes // 2, 768, 256), BF16),
        pltpu.VMEM((4 * GROUP, 8, 128), F32),
        pltpu.SMEM((8,), F32),
        pltpu.SMEM((2,), jnp.int32),
        pltpu.SemaphoreType.DMA((8,)),
        pltpu.SemaphoreType.DMA((8,)),
        pltpu.SemaphoreType.DMA((8,)),
        pltpu.SemaphoreType.DMA((4,)),
        pltpu.SemaphoreType.DMA((4,)),
    ]
    f, g, y, zt, r2, back = pl.pallas_call(
        kernel,
        out_shape=shapes,
        in_specs=[hbm] * 7,
        out_specs=[vmem] * 6,
        scratch_shapes=scratch,
        compiler_params=pltpu.CompilerParams(
            collective_id=0, has_side_effects=True, vmem_limit_bytes=54 << 20
        ),
    )(
        split_rows(distributions, grid_f),
        split_rows(gate_states, (3,) + plane),
        split_rows(history, (32,) + plane),
        split_rows(tissue, plane),
        split_rows(stim_site, plane),
        stim_amp,
        record_column,
    )
    parts = 8
    q, f, g, up = pl.pallas_call(
        basis_kernel,
        out_shape=[
            jax.ShapeDtypeStruct((32,) + plane, F32),
            jax.ShapeDtypeStruct(grid_f, F32),
            jax.ShapeDtypeStruct((3,) + plane, F32),
            jax.ShapeDtypeStruct((32, 32), F32),
        ],
        in_specs=[vmem] * 6,
        out_specs=[any_space] * 4,
        scratch_shapes=[
            pltpu.VMEM((32,) + plane, F32),
            pltpu.VMEM((32, 32), F32),
            pltpu.SemaphoreType.DMA((parts,)),
            pltpu.SemaphoreType.DMA((3,)),
        ],
        compiler_params=pltpu.CompilerParams(vmem_limit_bytes=48 << 20),
    )(y, f, g, zt, r2, back)
    return (
        join_rows(f, distributions.shape),
        join_rows(g, gate_states.shape),
        join_rows(q, history.shape),
        up,
    )


def solution(mesh):
    field = P(None, "slab", "tile", None)
    label = P("slab", "tile", None)
    return jax.shard_map(
        local,
        mesh=mesh,
        in_specs=(field, field, field, label, label, P(), P()),
        out_specs=(field, field, field, P()),
        check_vma=False,
    )
```

```python
import functools
import math

import jax
import jax.numpy as jnp
from jax import lax
from jax.experimental import pallas as pl
from jax.experimental.pallas import tpu as pltpu
from jax.sharding import PartitionSpec as P

MESH = pl.DeviceIdType.MESH
DT = 0.1
DEAD = -1e30
LIMIT = -1e29
F32 = jnp.float32
BF16 = jnp.bfloat16
NT = (((1,), (1,)), ((), ()))
GROUP = 16
PANEL = 16
STEP = 8


def split_rows(a, shape):
    lead = a.shape[:-2]
    a = jnp.swapaxes(a.reshape(lead + (4, 2, 128)), -3, -2)
    return a.reshape(shape)


def join_rows(a, shape):
    lead = shape[:-2]
    a = jnp.swapaxes(a.reshape(lead + (2, 4, 128)), -3, -2)
    return a.reshape(shape)


def typed(tissue):
    endo = tissue == 1
    mid = tissue == 2

    def pick(a, b, c):
        if a == b == c:
            return a
        if b == c:
            return jnp.where(endo, F32(a), F32(c))
        if a == c:
            return jnp.where(mid, F32(b), F32(c))
        if a == b:
            return jnp.where(tissue == 1, F32(a), jnp.where(mid, F32(a), F32(c)))
        return jnp.where(endo, F32(a), jnp.where(mid, F32(b), F32(c)))

    return pick


def each(fn, *columns):
    return tuple(fn(*entry) for entry in zip(*columns))


def collide(f, v, w, s, tissue, stim):
    pick = typed(tissue)
    live = tissue > 0
    u = ((f[0] + f[1]) + (f[2] + f[3])) + ((f[4] + f[5]) + f[6])
    hv = 0.5 + 0.5 * jnp.tanh(25.0 * (u - 0.3))
    hw = 0.5 + 0.5 * jnp.tanh(25.0 * (u - 0.13))
    hm = 0.5 + 0.5 * jnp.tanh(25.0 * (u - pick(0.2, 0.1, 0.006)))
    ho = 0.5 + 0.5 * jnp.tanh(25.0 * (u - pick(0.006, 0.005, 0.006)))
    nv, nw, no = 1.0 - hv, 1.0 - hw, 1.0 - ho
    tv1, tv2 = (75.0, 80.0, 60.0), (10.0, 1.4506, 1150.0)
    tvm = pick(*tv1) + hm * pick(*each(lambda a, b: b - a, tv1, tv2))
    tw1, tw2 = (6.0, 70.0, 60.0), (140.0, 8.0, 15.0)
    thw = jnp.tanh(pick(200.0, 200.0, 65.0) * (u - pick(0.016, 0.016, 0.03)))
    twm = pick(*each(lambda a, b: (a + b) / 2, tw1, tw2)) + thw * pick(
        *each(lambda a, b: (b - a) / 2, tw1, tw2)
    )
    ts1, ts2 = (40.0, 91.0, 30.0181), (1.2, 0.8, 0.9957)
    tht = jnp.tanh(pick(2.0, 2.1, 2.0458) * (u - pick(0.65, 0.6, 0.65)))
    tso = pick(*each(lambda a, b: (a + b) / 2, ts1, ts2)) + tht * pick(
        *each(lambda a, b: (b - a) / 2, ts1, ts2)
    )
    ts = 2.7342 + hw * pick(*each(lambda a: a - 2.7342, (2.0, 4.0, 16.0)))
    to1, to2 = (470.0, 410.0, 400.0), (6.0, 7.0, 6.0)
    to = pick(*to1) + ho * pick(*each(lambda a, b: b - a, to1, to2))
    winf = no * (1.0 - u * pick(*each(lambda a: 1 / a, (0.0273, 0.01, 0.07)))) + ho * pick(
        0.78, 0.5, 0.94
    )
    minus_fi = v * hv * (u - 0.3) * (pick(1.56, 1.61, 1.55) - u) * pick(
        *each(lambda a: 1 / a, (0.1, 0.078, 0.11))
    )
    outward = u * nw / to + hw / tso
    minus_si = hw * w * s * pick(*each(lambda a: 1 / a, (2.9013, 3.3849, 1.8875)))
    react = stim + minus_fi - outward + minus_si
    dv = nv * (1.0 - hm - v) / tvm - hv * v * (1 / 1.4506)
    dw = nw * (winf - w) / twm - hw * w * pick(*each(lambda a: 1 / a, (280.0, 280.0, 200.0)))
    ds = ((0.5 + 0.5 * jnp.tanh(2.0994 * (u - 0.9087))) - s) / ts
    gates = (
        jnp.where(live, v + DT * dv, v),
        jnp.where(live, w + DT * dw, w),
        jnp.where(live, s + DT * ds, s),
    )
    rate = pick(*each(lambda a: 1 / a, (0.95, 0.8, 1.1)))
    keep = pick(*each(lambda a: 1 - 1 / a, (0.95, 0.8, 1.1)))
    share = 0.125 * (u * rate + DT * react)
    g = [jnp.where(live, f[0] * keep + 2.0 * share, DEAD)]
    for i in range(1, 7):
        g.append(jnp.where(live, f[i] * keep + share, DEAD))
    return g, gates


def kernel(
    f_hbm, g_hbm, x_hbm, t_hbm, s_hbm, amp_hbm, rc_hbm,
    f_out, g_out, y_out, zt_ref, r2_ref, back_ref,
    fv, gv, xv, tv, sv, stim, cc, cxp, cxm, ysp, ysm, yrp, yrm, u1, u2,
    xs, red, amp, rc,
    load_sem, hs_sem, hr_sem, as_sem, ar_sem,
):
    planes = fv.shape[1]
    quads = planes // 4
    slabs, tiles = lax.axis_size("slab"), lax.axis_size("tile")
    slab, tile = lax.axis_index("slab"), lax.axis_index("tile")
    core, yy, zz = lax.rem(tile, 2), lax.rem(tile // 2, 4), tile // 8

    halves = [pl.ds(i * (planes // 2), planes // 2) for i in range(2)]
    loads = [
        pltpu.make_async_copy(src, dst, load_sem.at[i])
        for i, (src, dst) in enumerate(
            [(x_hbm.at[:, half], xv.at[:, half]) for half in halves]
            + [(f_hbm, fv), (t_hbm, tv), (s_hbm, sv), (g_hbm, gv), (amp_hbm, amp), (rc_hbm, rc)]
        )
    ]
    for copy in loads:
        copy.start()

    right = (lax.rem(slab + 1, slabs), tile)
    left = (lax.rem(slab + slabs - 1, slabs), tile)
    up = (slab, lax.rem(tile + 1, tiles))
    down = (slab, lax.rem(tile + tiles - 1, tiles))
    rank = (slab * 4 + yy, zz * 2 + core)

    def partner(stage, k):
        other = lax.rem(rank[stage] + k, GROUP)
        if stage == 0:
            return (other // 4, zz * 8 + lax.rem(other, 4) * 2 + core)
        return (slab, other // 2 * 8 + yy * 2 + lax.rem(other, 2))

    barrier = pltpu.get_barrier_semaphore()
    for dev in (right, left, up, down):
        pl.semaphore_signal(barrier, inc=1, device_id=dev, device_id_type=MESH)
    for stage in range(2):
        for k in range(1, GROUP):
            pl.semaphore_signal(barrier, inc=1, device_id=partner(stage, k), device_id_type=MESH)

    row4 = lax.broadcasted_iota(jnp.int32, (8, 128), 0)
    lane = lax.broadcasted_iota(jnp.int32, (4, 8, 128), 2)
    row = lax.broadcasted_iota(jnp.int32, (4, 8, 128), 1)
    yrow = lax.rem(row, 4)
    yrow2 = lax.rem(row4, 4)

    def store_collided(step, q, g):
        p = pl.ds(q * 4, 4)
        cc[0, p] = g[0]
        cc[1, p] = g[3]
        cc[2, p] = g[4]
        cc[3, p] = g[5]
        cc[4, p] = g[6]
        cxp[step, pl.ds(q * 4 + 1, 4)] = g[1]
        cxm[step, p] = g[2]
        face_p = g[3][3]
        face_m = g[4][0]
        for k in range(3):
            face_p = jnp.where(yrow2 == k, pltpu.roll(g[3][k], 5 + k, 0), face_p)
        for k in range(1, 4):
            face_m = jnp.where(yrow2 == k, pltpu.roll(g[4][k], k, 0), face_m)
        ysp[step, q] = face_p
        ysm[step, q] = face_m

    def halos(step):
        pairs = (
            (cxp.at[step, pl.ds(planes, 1)], cxp.at[step, pl.ds(0, 1)], right),
            (cxm.at[step, pl.ds(0, 1)], cxm.at[step, pl.ds(planes, 1)], left),
            (ysp.at[step], yrp.at[step], up),
            (ysm.at[step], yrm.at[step], down),
        )
        return [
            pltpu.make_async_remote_copy(
                src_ref=src,
                dst_ref=dst,
                send_sem=hs_sem.at[step * 4 + i],
                recv_sem=hr_sem.at[step * 4 + i],
                device_id=dev,
                device_id_type=MESH,
            )
            for i, (src, dst, dev) in enumerate(pairs)
        ]

    def settle_halos(step):
        for copy in halos(step):
            copy.wait_recv()
        cxp[step, pl.ds(0, 1)] = jnp.where(slab == 0, DEAD, cxp[step, pl.ds(0, 1)])
        cxm[step, pl.ds(planes, 1)] = jnp.where(
            slab == slabs - 1, DEAD, cxm[step, pl.ds(planes, 1)]
        )
        yrp[step] = jnp.where(tile == 0, DEAD, yrp[step])
        yrm[step] = jnp.where(tile == tiles - 1, DEAD, yrm[step])

    def propagate(step, q, tissue):
        p = pl.ds(q * 4, 4)
        p1 = pl.ds(q * 4 + 1, 4)

        def bounce(moved, back):
            return jnp.where(moved > LIMIT, moved, back)

        gx1, gx2 = cxp[step, p1], cxm[step, p]
        gy1, gy2, gz1, gz2 = cc[1, p], cc[2, p], cc[3, p], cc[4, p]
        hp, hm = yrp[step, q], yrm[step, q]
        halo_p = jnp.stack([hp] + [pltpu.roll(hp, 8 - k, 0) for k in range(1, 4)])
        halo_m = jnp.stack([pltpu.roll(hm, 3 - k, 0) for k in range(3)] + [hm])
        my1 = jnp.where(yrow == 0, halo_p, pltpu.roll(gy1, 1, 1))
        my2 = jnp.where(yrow == 3, halo_m, pltpu.roll(gy2, 7, 1))
        rz1 = pltpu.roll(gz1, 1, 2)
        rz2 = pltpu.roll(gz2, 127, 2)
        mz1 = jnp.where(lane == 0, jnp.where(row >= 4, pltpu.roll(rz1, 4, 1), DEAD), rz1)
        mz2 = jnp.where(lane == 127, jnp.where(row < 4, pltpu.roll(rz2, 4, 1), DEAD), rz2)
        f = (
            cc[0, p],
            bounce(cxp[step, p], gx2),
            bounce(cxm[step, p1], gx1),
            bounce(my1, gy2),
            bounce(my2, gy1),
            bounce(mz1, gz2),
            bounce(mz2, gz1),
        )
        live = tissue > 0
        f = [jnp.where(live, part, 0.0) for part in f]
        u = ((f[0] + f[1]) + (f[2] + f[3])) + ((f[4] + f[5]) + f[6])
        return f, u

    def advance(q, f, current, gates_to):
        p = pl.ds(q * 4, 4)
        g, gates = collide(f, gv[0, p], gv[1, p], gv[2, p], tv[p], current)
        for i in range(3):
            gates_to[i, p] = gates[i]
        return g

    def reduce_copy(which, stage, slot, k):
        return pltpu.make_async_remote_copy(
            src_ref=slot,
            dst_ref=slot,
            send_sem=as_sem.at[which * 2 + stage],
            recv_sem=ar_sem.at[which * 2 + stage],
            device_id=partner(stage, k),
            device_id_type=MESH,
        )

    def reduce_send(which, stage, block):
        at = (which * 2 + stage) * GROUP + rank[stage]
        red[at] = block
        for k in range(1, GROUP):
            reduce_copy(which, stage, red.at[at], k).start()

    def reduce_all(which, stage):
        return reduce_copy(
            which, stage, red.at[pl.ds((which * 2 + stage) * GROUP, GROUP - 1)], 1
        )

    def reduce_sum(which, stage):
        reduce_all(which, stage).wait_recv()
        at = (which * 2 + stage) * GROUP
        parts = [red[at + i] for i in range(GROUP)]
        while len(parts) > 1:
            parts = [a + b for a, b in zip(parts[::2], parts[1::2])]
        return parts[0]

    def packed(m):
        return jnp.concatenate([m[8 * b : 8 * b + 8] for b in range(4)], axis=1)

    def unpacked(m):
        return jnp.concatenate([m[:, 32 * b : 32 * b + 32] for b in range(4)], axis=0)

    ri = lax.broadcasted_iota(jnp.int32, (32, 32), 0)
    ci = lax.broadcasted_iota(jnp.int32, (32, 32), 1)

    eye = jnp.where(ri == ci, 1.0, 0.0)

    def eliminate(a):
        m = jnp.concatenate([a, eye], axis=1)
        below = lax.broadcasted_iota(jnp.int32, (32, 64), 0)
        for p in range(0, 32, PANEL):
            cols = [jnp.broadcast_to(m[:, p + k : p + k + 1], (32, 64)) for k in range(PANEL)]
            rows = [m[p + k : p + k + 1, :] for k in range(PANEL)]
            taken_off = 0.0
            for k in range(PANEL):
                j = p + k
                low = jnp.where(below > j, cols[k] * (1.0 / cols[k][j : j + 1, :]), 0.0)
                for q in range(k + 1, PANEL):
                    cols[q] = cols[q] - low * cols[q][j : j + 1, :]
                    rows[q] = rows[q] - low[p + q : p + q + 1, :] * rows[k]
                taken_off = taken_off + low * rows[k]
            m = m - taken_off
        upper = m[:, :32]
        pivot = jnp.sum(jnp.where(ri == ci, upper, 0.0), axis=1, keepdims=True)
        return jnp.where(ri <= ci, upper, 0.0), m[:, 32:], pivot

    wide_row = lax.broadcasted_iota(jnp.int32, (256, 256), 0)
    wide_col = lax.broadcasted_iota(jnp.int32, (256, 256), 1)
    same = lax.rem(wide_row, 8) == lax.rem(wide_col, 8)

    def folded(p):
        m = jnp.sum(jnp.where(same, p, 0.0).reshape(32, 8, 256), axis=1)
        place = lax.broadcasted_iota(jnp.int32, (256, 32), 0) // 8
        pick = jnp.where(place == lax.broadcasted_iota(jnp.int32, (256, 32), 1), 1.0, 0.0)
        return jnp.dot(m, pick, precision=lax.Precision.HIGHEST, preferred_element_type=F32)


    def pair(x):
        return jnp.concatenate([xv[:, 2 * x].reshape(256, 128), xv[:, 2 * x + 1].reshape(256, 128)], axis=1)

    def old_gram(i, acc):
        parts = [pair(STEP * i + k).astype(BF16) for k in range(STEP)]
        for k in range(STEP):
            xs[STEP * i + k, :256] = parts[k]
        hi = jnp.concatenate(parts, axis=1)
        return acc + lax.dot_general(hi, hi, NT, preferred_element_type=F32)

    share = planes // 4 // STEP
    acc = jnp.zeros((256, 256), F32)
    for half in range(2):
        loads[half].wait()
        acc = lax.fori_loop(half * share, (half + 1) * share, old_gram, acc)
    block = packed(folded(acc))
    pl.semaphore_wait(barrier, 4 + 2 * (GROUP - 1))
    reduce_send(0, 0, block)

    for copy in loads[2:]:
        copy.wait()

    def first(q, carry):
        p = pl.ds(q * 4, 4)
        site = sv[p]
        current = jnp.zeros((4, 8, 128), F32)
        for k in range(8):
            current = jnp.where(site == k + 1, amp[k], current)
        stim[p] = current
        store_collided(0, q, advance(q, [fv[i, p] for i in range(7)], current, gv))
        return carry

    lax.fori_loop(0, quads, first, 0)
    for copy in halos(0):
        copy.start()

    def finer(i, carry):
        rest = pair(i) - xs[i, :256].astype(F32)
        mid = rest.astype(BF16)
        xs[i, 256:512] = mid
        xs[i, 512:] = (rest - mid.astype(F32)).astype(BF16)
        return carry

    lax.fori_loop(0, planes // 2, finer, 0)

    reduce_send(0, 1, reduce_sum(0, 0))

    settle_halos(0)

    def second(q, carry):
        p = pl.ds(q * 4, 4)
        f, u = propagate(0, q, tv[p])
        u1[p] = u
        store_collided(1, q, advance(q, f, stim[p], g_out))
        return carry

    lax.fori_loop(0, quads, second, 0)
    for copy in halos(1):
        copy.start()

    settle_halos(1)

    def fourth(q, carry):
        p = pl.ds(q * 4, 4)
        f, u = propagate(1, q, tv[p])
        u2[p] = u
        for i in range(7):
            f_out[i, p] = f[i]
        return carry

    lax.fori_loop(0, quads, fourth, 0)

    gram = unpacked(reduce_sum(0, 1))
    taken = (ri == rc[0]) | (ri == rc[1]) | (ci == rc[0]) | (ci == rc[1])
    gram = jnp.where(taken, eye, gram * (1.0 + eye * 2.0**-16))
    _, inv0, pivot = eliminate(gram)
    t0 = (inv0 * (1.0 / jnp.sqrt(pivot))).astype(BF16)
    spread = spread_rows(t0, True, False)
    spread = jnp.concatenate([spread, spread, spread], axis=1)

    column = lax.broadcasted_iota(jnp.int32, (32, 256), 0)
    is1, is2 = column == rc[0], column == rc[1]

    def new_gram(i, acc):
        his, los = [], []
        for k in range(STEP):
            at = STEP * i + k
            y = jnp.dot(spread, xs[at], preferred_element_type=F32)
            new1 = jnp.concatenate([u1[2 * at], u1[2 * at + 1]], axis=1)
            new2 = jnp.concatenate([u2[2 * at], u2[2 * at + 1]], axis=1)
            for r in range(8):
                part = y[32 * r : 32 * r + 32]
                part = jnp.where(is2, new2[r : r + 1], part)
                part = jnp.where(is1, new1[r : r + 1], part)
                hi = part.astype(BF16)
                lo = (part - hi.astype(F32)).astype(BF16)
                y_out[at, 0, 32 * r : 32 * r + 32] = hi
                y_out[at, 1, 32 * r : 32 * r + 32] = lo
                his.append(hi)
                los.append(lo)
        both = jnp.concatenate(
            [jnp.concatenate(his, axis=1), jnp.concatenate(los, axis=1)], axis=0
        )
        return acc + lax.dot_general(both, both, NT, preferred_element_type=F32)

    acc = lax.fori_loop(0, planes // 2 // STEP, new_gram, jnp.zeros((64, 64), F32))
    gram = acc[:32, :32] + ((acc[:32, 32:] + acc[32:, :32]) + acc[32:, 32:])
    reduce_send(1, 0, packed(gram))
    _, inv0, pivot = eliminate(t0.astype(F32))
    back_ref[...] = inv0 * (1.0 / pivot)
    reduce_send(1, 1, reduce_sum(1, 0))
    r2, inv2, pivot = eliminate(unpacked(reduce_sum(1, 1)))
    scale = 1.0 / jnp.sqrt(pivot)
    norm = math.sqrt(planes * 1024 * slabs * tiles)
    zt_ref[...] = inv2 * (scale * norm)
    r2_ref[...] = r2 * (scale * (1.0 / norm))

    for step in range(2):
        for copy in halos(step):
            copy.wait_send()
    for which in range(2):
        for stage in range(2):
            reduce_all(which, stage).wait_send()


def places(shape, dim, row_first):
    at = lax.broadcasted_iota(jnp.int32, shape, dim)
    return (at // 32, lax.rem(at, 32)) if row_first else (lax.rem(at, 8), at // 8)


def spread_rows(t, out_row_first, in_row_first):
    index = lax.broadcasted_iota(jnp.int32, (256, 32), 1)

    def pick(row_first):
        return jnp.where(places((256, 32), 0, row_first)[1] == index, 1.0, 0.0).astype(BF16)

    half = jnp.dot(pick(out_row_first), t, preferred_element_type=F32).astype(BF16)
    full = lax.dot_general(half, pick(in_row_first), NT, preferred_element_type=F32)
    same = places((256, 256), 0, out_row_first)[0] == places((256, 256), 1, in_row_first)[0]
    return jnp.where(same, full, 0.0).astype(BF16)


def basis_kernel(
    y_ref, f_ref, g_ref, z_ref, r2_ref, back_ref,
    q_hbm, f_hbm, g_hbm, up_hbm, qv, up, q_sem, p_sem,
):
    parts = q_sem.shape[0]
    pairs = y_ref.shape[0] // parts
    passed = [
        pltpu.make_async_copy(src, dst, p_sem.at[i])
        for i, (src, dst) in enumerate(((f_ref, f_hbm), (g_ref, g_hbm), (up, up_hbm)))
    ]
    for copy in passed[:2]:
        copy.start()
    z = z_ref[...]
    hi = z.astype(BF16)
    spread = spread_rows(hi, False, True)
    rest = spread_rows((z - hi.astype(F32)).astype(BF16), False, True)
    wide = jnp.concatenate([spread, spread, rest], axis=1)
    stores = []
    for i in range(parts):
        for k in range(pairs):
            at = i * pairs + k
            tall = jnp.concatenate([y_ref[at, 0], y_ref[at, 1], y_ref[at, 0]], axis=0)
            q = jnp.dot(wide, tall, preferred_element_type=F32)
            for j in range(2):
                qv[:, 2 * at + j] = q[:, 128 * j : 128 * j + 128].reshape(32, 8, 128)
        planes = pl.ds(2 * i * pairs, 2 * pairs)
        stores.append(
            pltpu.make_async_copy(qv.at[:, planes], q_hbm.at[:, planes], q_sem.at[i])
        )
        stores[-1].start()
        if i == parts // 2:
            up[...] = lax.dot_general(
                r2_ref[...],
                back_ref[...],
                NT,
                precision=lax.Precision.HIGHEST,
                preferred_element_type=F32,
            )
            passed[2].start()
    for copy in passed + stores:
        copy.wait()


def local(distributions, gate_states, history, tissue, stim_site, stim_amp, record_column):
    planes = distributions.shape[1]
    hbm = pl.BlockSpec(memory_space=pltpu.HBM)
    any_space = pl.BlockSpec(memory_space=pl.ANY)
    vmem = pl.BlockSpec(memory_space=pltpu.VMEM)
    grid_f = (7, planes, 8, 128)
    shapes = [
        pltpu.VMEM(grid_f, F32),
        pltpu.VMEM((3, planes, 8, 128), F32),
        pltpu.VMEM((planes // 2, 2, 256, 256), BF16),
        pltpu.VMEM((32, 32), F32),
        pltpu.VMEM((32, 32), F32),
        pltpu.VMEM((32, 32), F32),
    ]
    plane = (planes, 8, 128)
    scratch = [
        pltpu.VMEM(grid_f, F32),
        pltpu.VMEM((3,) + plane, F32),
        pltpu.VMEM((32,) + plane, F32),
        pltpu.VMEM(plane, jnp.int32),
        pltpu.VMEM(plane, jnp.int32),
        pltpu.VMEM(plane, F32),
        pltpu.VMEM((5,) + plane, F32),
        pltpu.VMEM((2, planes + 1, 8, 128), F32),
        pltpu.VMEM((2, planes + 1, 8, 128), F32),
        pltpu.VMEM((2, planes // 4, 8, 128), F32),
        pltpu.VMEM((2, planes // 4, 8, 128), F32),
        pltpu.VMEM((2, planes // 4, 8, 128), F32),
        pltpu.VMEM((2, planes // 4, 8, 128), F32),
        pltpu.VMEM(plane, F32),
        pltpu.VMEM(plane, F32),
        pltpu.VMEM((planes // 2, 768, 256), BF16),
        pltpu.VMEM((4 * GROUP, 8, 128), F32),
        pltpu.SMEM((8,), F32),
        pltpu.SMEM((2,), jnp.int32),
        pltpu.SemaphoreType.DMA((8,)),
        pltpu.SemaphoreType.DMA((8,)),
        pltpu.SemaphoreType.DMA((8,)),
        pltpu.SemaphoreType.DMA((4,)),
        pltpu.SemaphoreType.DMA((4,)),
    ]
    f, g, y, zt, r2, back = pl.pallas_call(
        kernel,
        out_shape=shapes,
        in_specs=[hbm] * 7,
        out_specs=[vmem] * 6,
        scratch_shapes=scratch,
        compiler_params=pltpu.CompilerParams(
            collective_id=0, has_side_effects=True, vmem_limit_bytes=54 << 20
        ),
    )(
        split_rows(distributions, grid_f),
        split_rows(gate_states, (3,) + plane),
        split_rows(history, (32,) + plane),
        split_rows(tissue, plane),
        split_rows(stim_site, plane),
        stim_amp,
        record_column,
    )
    parts = 8
    q, f, g, up = pl.pallas_call(
        basis_kernel,
        out_shape=[
            jax.ShapeDtypeStruct((32,) + plane, F32),
            jax.ShapeDtypeStruct(grid_f, F32),
            jax.ShapeDtypeStruct((3,) + plane, F32),
            jax.ShapeDtypeStruct((32, 32), F32),
        ],
        in_specs=[vmem] * 6,
        out_specs=[any_space] * 4,
        scratch_shapes=[
            pltpu.VMEM((32,) + plane, F32),
            pltpu.VMEM((32, 32), F32),
            pltpu.SemaphoreType.DMA((parts,)),
            pltpu.SemaphoreType.DMA((3,)),
        ],
        compiler_params=pltpu.CompilerParams(vmem_limit_bytes=48 << 20),
    )(y, f, g, zt, r2, back)
    return (
        join_rows(f, distributions.shape),
        join_rows(g, gate_states.shape),
        join_rows(q, history.shape),
        up,
    )


def solution(mesh):
    field = P(None, "slab", "tile", None)
    label = P("slab", "tile", None)
    return jax.shard_map(
        local,
        mesh=mesh,
        in_specs=(field, field, field, label, label, P(), P()),
        out_specs=(field, field, field, P()),
        check_vma=False,
    )
```
